256 devices in a mesh: pole: 8 (over y, core), snode: 32 (over x, z).
Axes of the slice: x: 4, y: 4, z: 8, core: 2. Of those that a mesh axis runs over, the one named last changes fastest.
Arguments:
- pivot_inverse: float32 [16, 64, 2, 256, 256], P('pole', 'snode'), as said below
- factor_block: float32 [16, 64, 2, 256, 256], P('pole', 'snode')
- live_width_array: int32 [64], P('snode'), may hold values from 128 to 256, as said below
- pole_weight: float32 [16, 2], P('pole'), may hold values from -4 to 4
Outputs:
- density_diag: float32 [64, 256, 256], P('snode')
- density_off: float32 [64, 256, 256], P('snode')
The draws below stay inside these ranges and needn't reach their ends.
Inputs may be any that keep to these rules, and one draw needn't show every extreme that they name: `live_width_array`: live widths of the supernodes; at least one supernode is 256 wide and one is 128 wide. `pivot_inverse`: symmetric in its last two dimensions with a dominant real diagonal.
All inputs are finite; a program needn't handle non-finite values.
Results may differ from the reference program's by a relative error of at most 0.0003.
Values sent between devices are 32-bit elements; how exact they have to be, the bound alone decides.
A program may use at most 192 MiB of HBM per device.

```python
import jax
import jax.numpy as jnp
from jax import lax

W = 256
CLUSTER_COUNT = 64
RESIDUE_COUNT = 16


def draw_pivot_inverse(key, part):
    key = jax.random.fold_in(key, 12)
    first, second = jax.random.split(key)
    noise = jax.random.normal(first, (RESIDUE_COUNT, CLUSTER_COUNT, 2, W, W), jnp.float32)
    noise = noise * (0.35 / W ** 0.5)
    symmetric = (noise + jnp.swapaxes(noise, -1, -2)) * 0.7071
    gains = jax.random.uniform(second, (RESIDUE_COUNT, CLUSTER_COUNT, 1, W), jnp.float32, 0.6, 1.4)
    unit_matrix = jnp.eye(W, dtype=jnp.float32)
    diagonal = unit_matrix[None, None, :, :] * gains
    parts_flag = jnp.array([1.0, 0.0], jnp.float32)[None, None, :, None, None]
    return symmetric + parts_flag * diagonal[:, :, None, :, :]


def draw_factor_block(key, part):
    key = jax.random.fold_in(key, 11)
    first, second, third, quartic_coefficient = jax.random.split(key, 4)
    low_rate = 0.3 / CLUSTER_COUNT
    high_rate = 0.08
    noise = jax.random.normal(first, (RESIDUE_COUNT, CLUSTER_COUNT, 2, W, W), jnp.float32)
    noise = noise * (0.15 / W ** 0.5)
    base_rate = jnp.exp(jax.random.uniform(second, (RESIDUE_COUNT, 1, W), jnp.float32, jnp.log(low_rate), jnp.log(high_rate)))
    wobble = jnp.exp(jax.random.uniform(third, (RESIDUE_COUNT, CLUSTER_COUNT, 1), jnp.float32, -0.5, 0.5))
    spike_magnitude = jax.random.uniform(quartic_coefficient, (RESIDUE_COUNT, CLUSTER_COUNT, 1), jnp.float32) < 3.0 / CLUSTER_COUNT
    objective_scalar = jnp.where(spike_magnitude, 0.6, 1.0)
    diagonal_values = jnp.exp(-base_rate * wobble) * objective_scalar
    unit_matrix = jnp.eye(W, dtype=jnp.float32)
    diagonal = unit_matrix[None, None, :, :] * diagonal_values[:, :, None, :]
    parts_flag = jnp.array([1.0, 0.0], jnp.float32)[None, None, :, None, None]
    return noise + parts_flag * diagonal[:, :, None, :, :]


def draw_live_width_array(key, part):
    key = jax.random.fold_in(key, 13)
    first, second, third = jax.random.split(key, 3)
    widths = jax.random.randint(first, (CLUSTER_COUNT,), W // 2, W + 1, jnp.int32)
    widest_width = jax.random.randint(second, (), 0, CLUSTER_COUNT, jnp.int32)
    narrow = (widest_width + 1 + jax.random.randint(third, (), 0, CLUSTER_COUNT - 1, jnp.int32)) % CLUSTER_COUNT
    widths = widths.at[widest_width].set(W)
    widths = widths.at[narrow].set(W // 2)
    return widths


def shard_levels(rng, dims, shards, least, largest):
    gain, own = 1.0, jax.random.fold_in(rng, 6)
    for dim, blocks in shards:
        steps = jnp.exp(jax.random.uniform(jax.random.fold_in(own, dim), (blocks,), jnp.float32, least / len(shards), largest / len(shards)))
        gain = gain * jnp.repeat(steps, dims[dim] // blocks).reshape([-1 if axis == dim else 1 for axis in range(len(dims))])
    return gain


def normal_values(key, extent, scale, bound, pieces=(), kind=jnp.bfloat16):
    entries = scale * jax.random.normal(key, extent, jnp.float32)
    if pieces:
        entries = entries * shard_levels(key, extent, pieces, -0.22, 0.18)
    return jnp.clip(entries, -bound, bound).astype(kind)


def setup_inputs(seed: int = 0) -> dict:
    splits = jax.random.split(jax.random.key(seed), 5)
    return {
        "pivot_inverse": draw_pivot_inverse(jax.random.fold_in(splits[4], 71), 0),
        "factor_block": draw_factor_block(jax.random.fold_in(splits[4], 71), 0),
        "live_width_array": draw_live_width_array(jax.random.fold_in(splits[4], 71), 0),
        "pole_weight": normal_values(splits[3], (RESIDUE_COUNT, 2), 1.0, 4.0, ((0, 8),), jnp.float32),
    }


def multiply_real(left, right):
    return jnp.einsum("...ij,...jk->...ik", left, right, precision=lax.Precision.HIGHEST)


def complex_product(left, right):
    left_real = left[..., 0, :, :]
    leading_imaginary = left[..., 1, :, :]
    right_re = right[..., 0, :, :]
    right_im = right[..., 1, :, :]
    real_part = multiply_real(left_real, right_re) - multiply_real(leading_imaginary, right_im)
    imag_part = multiply_real(left_real, right_im) + multiply_real(leading_imaginary, right_re)
    return jnp.stack([real_part, imag_part], axis=-3)


def transpose_block(block):
    return jnp.swapaxes(block, -1, -2)


def reference(pivot_inverse, factor_block, live_width_array, pole_weight):
    columns = jnp.arange(W, dtype=jnp.int32)
    keep = (columns[None, :] < live_width_array[:, None]).astype(jnp.float32)
    pivot = pivot_inverse * keep[None, :, None, :, None] * keep[None, :, None, None, :]
    factor = factor_block * keep[None, :, None, None, :]

    def one_pole(inputs):
        pole_pivot, pole_factor, weight = inputs

        def proceed_upward(parent, blocks):
            diag_block, link = blocks
            product = complex_product(parent, link)
            inverse = diag_block + complex_product(transpose_block(link), product)
            return inverse, (inverse, -product)

        start = jnp.zeros((2, W, W), jnp.float32)
        _, (reciprocal_matrices, offsets) = lax.scan(proceed_upward, start, (pole_pivot, pole_factor))
        diag_part = weight[0] * reciprocal_matrices[:, 1] + weight[1] * reciprocal_matrices[:, 0]
        off_part = weight[0] * offsets[:, 1] + weight[1] * offsets[:, 0]
        return diag_part, off_part

    diag_terms, off_terms = lax.map(one_pole, (pivot, factor, pole_weight))
    return jnp.sum(diag_terms, axis=0), jnp.sum(off_terms, axis=0)
```

```python
import functools

import jax
import jax.numpy as jnp
from jax import lax
from jax.experimental import pallas as pl
from jax.experimental.pallas import tpu as pltpu
from jax.sharding import PartitionSpec as P

MESH = pl.DeviceIdType.MESH
F32 = jnp.float32
BF = jnp.bfloat16
W = 256
H = 128
PACK = 264
PART = 104
ROWS = 8 * PART
CHUNKS = 4
CROWS = W // CHUNKS
GROUP = 4


def split(x):
    high = x.astype(BF)
    return high, (x - high.astype(F32)).astype(BF)


def csplit(pair):
    return split(pair[0]) + split(pair[1])


def dot(a, b):
    return jnp.dot(a, b, preferred_element_type=F32)


def dot_t(a, b):
    return lax.dot_general(a, b, (((0,), (0,)), ((), ())), preferred_element_type=F32)


def product(left, right, mul=dot):
    lrh, lrl, lih, lil = left
    rrh, rrl, rih, ril = right
    real = mul(lrh, rrh) - mul(lih, rih)
    real += (mul(lrl, rrh) + mul(lrh, rrl)) - (mul(lil, rih) + mul(lih, ril))
    imag = mul(lrh, rih) + mul(lih, rrh)
    imag += (mul(lrl, rih) + mul(lrh, ril)) + (mul(lil, rrh) + mul(lih, rrl))
    return real, imag


def sandwich(middle, outer):
    return product(outer, csplit(product(csplit(middle), outer)), dot_t)


def tri():
    row = lax.broadcasted_iota(jnp.int32, (H, H), 0)
    col = lax.broadcasted_iota(jnp.int32, (H, H), 1)
    return row, col


def pack_into(ref, block):
    row, col = tri()
    last = block[H:, H:]
    ref[0:H, :] = block[:H, H:]
    ref[H : 2 * H, :] = jnp.where(row <= col, block[:H, :H], last)
    diagonal = jnp.sum(jnp.where(row == col, last, 0.0), axis=0, keepdims=True)
    ref[2 * H : PACK, :] = jnp.broadcast_to(diagonal, (8, H))


def unpack(ref):
    row, col = tri()
    upper = ref[0:H, :]
    both = ref[H : 2 * H, :]
    both_t = both.T
    diagonal = ref[2 * H : 2 * H + 1, :]
    first = jnp.where(row <= col, both, both_t)
    last = jnp.where(row > col, both, jnp.where(row == col, diagonal, both_t))
    return jnp.concatenate(
        [jnp.concatenate([first, upper], 1), jnp.concatenate([upper.T, last], 1)], 0
    )


def unpack2(ref):
    return unpack(ref.at[0]), unpack(ref.at[1])


def pack2(ref, pair):
    pack_into(ref.at[0], pair[0])
    pack_into(ref.at[1], pair[1])


def kernel(
    nodes,
    width_ref,
    weight_ref,
    p_ref,
    f_ref,
    diag_ref,
    off_ref,
    fs,
    a_s,
    b_own,
    a_ex,
    a_exs,
    a_in,
    a_ins,
    b_ex,
    b_in,
    b_full,
    s_got,
    s_out,
    s_in,
    dens,
    parts,
    total,
    spare,
    b_send,
    b_recv,
    a_send,
    a_recv,
    s_send,
    s_recv,
    rs_send,
    rs_recv,
    ag_send,
    ag_recv,
):
    me = lax.axis_index("pole")
    i = lax.axis_index("snode")
    groups = nodes // GROUP
    g = lax.rem(i, GROUP)
    m = lax.div(i, GROUP)
    head = g == GROUP - 1
    poles = range(2)

    barrier = pltpu.get_barrier_semaphore()
    for step in range(1, GROUP + 1):
        for near in (lax.rem(i + step, nodes), lax.rem(i + nodes - step, nodes)):
            pl.semaphore_signal(barrier, inc=1, device_id=(me, near), device_id_type=MESH)
    for step in range(1, 8):
        pl.semaphore_signal(
            barrier, inc=1, device_id=(lax.rem(me + step, 8), i), device_id_type=MESH
        )

    row = lax.broadcasted_iota(jnp.int32, (W, W), 0)
    col = lax.broadcasted_iota(jnp.int32, (W, W), 1)

    def pivot(p, k):
        live = (row < width_ref[k]) & (col < width_ref[k])
        return tuple(jnp.where(live, p_ref[p, k, part], 0.0) for part in range(2))

    def load4(ref):
        return tuple(ref[n] for n in range(4))

    def store4(ref, four):
        for n in range(4):
            ref[n] = four[n]

    def send_b(p):
        return pltpu.make_async_remote_copy(
            src_ref=b_in.at[p],
            dst_ref=b_ex.at[p],
            send_sem=b_send.at[p],
            recv_sem=b_recv.at[p],
            device_id=(me, lax.rem(i + 1, nodes)),
            device_id_type=MESH,
        )

    def send_a(p, c):
        rows = pl.ds(c * CROWS, CROWS)
        return pltpu.make_async_remote_copy(
            src_ref=a_in.at[p, :, rows],
            dst_ref=a_ex.at[p, :, rows],
            send_sem=a_send.at[p, c],
            recv_sem=a_recv.at[p, c],
            device_id=(me, lax.rem(i + 1, nodes)),
            device_id_type=MESH,
        )

    def send_s(p, ahead, src):
        return pltpu.make_async_remote_copy(
            src_ref=src.at[p],
            dst_ref=s_got.at[p],
            send_sem=s_send.at[p, ahead - 1],
            recv_sem=s_recv.at[p],
            device_id=(me, lax.rem(i + ahead, nodes)),
            device_id_type=MESH,
        )

    def send_state(p, src):
        for ahead in (GROUP,) + tuple(range(1, GROUP)):
            send_s(p, ahead, src).start()

    for p in poles:
        for k in range(2):
            live = col < width_ref[k]
            store4(
                fs.at[p, k],
                csplit([jnp.where(live, f_ref[p, k, part], 0.0) for part in range(2)]),
            )
        outer = load4(fs.at[p, 1])
        inner = sandwich(pivot(p, 0), outer)
        last = pivot(p, 1)
        for part in range(2):
            b_own[p, part] = last[part] + inner[part]

        @pl.when(g == 0)
        def _():
            pack2(b_in.at[p], (b_own[p, 0], b_own[p, 1]))

        if p == 0:
            pl.semaphore_wait(barrier, 2 * GROUP + 7)

        @pl.when(g == 0)
        def _():
            send_b(p).start()

    for p in poles:
        real, imag = product(load4(fs.at[p, 0]), load4(fs.at[p, 1]))
        store4(a_s.at[p], csplit((real, imag)))

        @pl.when((g == 0) & (m > 0))
        def _():
            a_in[p, 0] = real
            a_in[p, 1] = imag
            for c in range(CHUNKS):
                send_a(p, c).start()

    @pl.when(g > 0)
    def _():
        for p in poles:
            send_b(p).wait_recv()
            outer = load4(a_s.at[p])
            inner = sandwich(unpack2(b_ex.at[p]), outer)
            full = (b_own[p, 0] + inner[0], b_own[p, 1] + inner[1])
            pack2(b_in.at[p], full)

            @pl.when(~head)
            def _():
                send_b(p).start()

            @pl.when(head & (m == 0))
            def _():
                send_state(p, b_in)

            b_full[p, 0] = full[0]
            b_full[p, 1] = full[1]

    @pl.when((g > 0) & (m > 0))
    def _():
        for p in poles:
            outer = load4(a_s.at[p])
            for c in range(CHUNKS):
                rows = pl.ds(c * CROWS, CROWS)
                send_a(p, c).wait_recv()
                left = csplit((a_ex[p, 0, rows], a_ex[p, 1, rows]))
                for n in range(4):
                    a_exs[p, n, rows] = left[n]
                real, imag = product(left, outer)

                @pl.when(~head)
                def _():
                    a_in[p, 0, rows] = real
                    a_in[p, 1, rows] = imag
                    send_a(p, c).start()

                @pl.when(head)
                def _():
                    four = csplit((real, imag))
                    for n in range(4):
                        a_ins[p, n, rows] = four[n]

    @pl.when(m > 0)
    def _():
        for p in poles:
            send_s(p, 1, s_out).wait_recv()

            @pl.when(head & (m < groups - 1))
            def _():
                inner = sandwich(unpack2(s_got.at[p]), load4(a_ins.at[p]))
                pack2(s_out.at[p], (b_full[p, 0] + inner[0], b_full[p, 1] + inner[1]))
                send_state(p, s_out)

    def send_part(k, step):
        to = lax.rem(me + step, 8)
        return pltpu.make_async_remote_copy(
            src_ref=dens.at[k, pl.ds(pl.multiple_of(to * PART, 8), PART)],
            dst_ref=parts.at[k, step - 1],
            send_sem=rs_send.at[k, step - 1],
            recv_sem=rs_recv.at[k, step - 1],
            device_id=(to, i),
            device_id_type=MESH,
        )

    def send_total(k, step):
        to = lax.rem(me + step, 8)
        rows = pl.ds(pl.multiple_of(me * PART, 8), PART)
        return pltpu.make_async_remote_copy(
            src_ref=total.at[k, rows],
            dst_ref=total.at[k, rows],
            send_sem=ag_send.at[k, step - 1],
            recv_sem=ag_recv.at[k, step - 1],
            device_id=(to, i),
            device_id_type=MESH,
        )

    order = (4, 3, 5, 2, 6, 7, 1)

    def put(p, k, product_pair, inverse_pair):
        re_w, im_w = weight_ref[p, 0], weight_ref[p, 1]
        off = -(re_w * product_pair[1] + im_w * product_pair[0])
        diag = re_w * inverse_pair[1] + im_w * inverse_pair[0]
        mine = dens.at[k]
        if p == 0:
            mine[0:W, :] = off[:, :H]
            mine[W : 2 * W, :] = off[:, H:]
            pack_into(mine.at[pl.ds(2 * W, PACK)], diag)
            mine[2 * W + PACK : ROWS, :] = jnp.zeros((ROWS - 2 * W - PACK, H), F32)
        else:
            mine[0:W, :] += off[:, :H]
            mine[W : 2 * W, :] += off[:, H:]
            pack_into(spare, diag)
            mine[2 * W : 2 * W + PACK, :] += spare[...]
            for step in order:
                send_part(k, step).start()

    for p in poles:

        @pl.when(m == 0)
        def _():
            @pl.when(g == 0)
            def _():
                s_in[...] = jnp.zeros_like(s_in)

            @pl.when(g > 0)
            def _():
                got = unpack2(b_ex.at[p])
                s_in[0] = got[0]
                s_in[1] = got[1]

        @pl.when(m > 0)
        def _():
            got = unpack2(s_got.at[p])

            @pl.when(g == 0)
            def _():
                s_in[0] = got[0]
                s_in[1] = got[1]

            @pl.when(g > 0)
            def _():
                inner = sandwich(got, load4(a_exs.at[p]))
                base = unpack2(b_ex.at[p])
                s_in[0] = base[0] + inner[0]
                s_in[1] = base[1] + inner[1]

        state = (s_in[0], s_in[1])
        for k in range(2):
            link = load4(fs.at[p, k])
            moved = product(csplit(state), link)
            inner = product(link, csplit(moved), dot_t)
            block = pivot(p, k)
            state = (block[0] + inner[0], block[1] + inner[1])
            put(p, k, moved, state)

    mine = pl.ds(pl.multiple_of(me * PART, 8), PART)
    for k in range(2):
        acc = dens[k, mine]
        for step in range(1, 8):
            send_part(k, step).wait_recv()
            acc = acc + parts[k, step - 1]
        total[k, mine] = acc
        for step in order:
            send_total(k, step).start()
    for k in range(2):
        for step in range(1, 8):
            back = lax.rem(me + 8 - step, 8)
            rows = pl.ds(pl.multiple_of(back * PART, 8), PART)
            pltpu.make_async_remote_copy(
                src_ref=total.at[k, rows],
                dst_ref=total.at[k, rows],
                send_sem=ag_send.at[k, step - 1],
                recv_sem=ag_recv.at[k, step - 1],
                device_id=(back, i),
                device_id_type=MESH,
            ).wait_recv()
        off_ref[k, :, 0:H] = total[k, 0:W]
        off_ref[k, :, H:W] = total[k, W : 2 * W]
        diag_ref[k] = unpack(total.at[k, pl.ds(2 * W, PACK)])

    for p in poles:

        @pl.when(~head)
        def _():
            send_b(p).wait_send()

        @pl.when(~head & (m > 0))
        def _():
            for c in range(CHUNKS):
                send_a(p, c).wait_send()

        @pl.when(head & (m < groups - 1))
        def _():
            for ahead in range(1, GROUP + 1):
                send_s(p, ahead, s_out).wait_send()

    for k in range(2):
        for step in range(1, 8):
            send_part(k, step).wait_send()
            send_total(k, step).wait_send()


def local(nodes, pivot_inverse, factor_block, live_width_array, pole_weight):
    vmem = pl.BlockSpec(memory_space=pltpu.VMEM)
    smem = pl.BlockSpec(memory_space=pltpu.SMEM)
    dma = pltpu.SemaphoreType.DMA
    return pl.pallas_call(
        functools.partial(kernel, nodes),
        out_shape=[jax.ShapeDtypeStruct((2, W, W), F32)] * 2,
        in_specs=[smem, smem, vmem, vmem],
        out_specs=[vmem, vmem],
        scratch_shapes=[
            pltpu.VMEM((2, 2, 4, W, W), BF),
            pltpu.VMEM((2, 4, W, W), BF),
            pltpu.VMEM((2, 2, W, W), F32),
            pltpu.VMEM((2, 2, W, W), F32),
            pltpu.VMEM((2, 4, W, W), BF),
            pltpu.VMEM((2, 2, W, W), F32),
            pltpu.VMEM((2, 4, W, W), BF),
            pltpu.VMEM((2, 2, PACK, H), F32),
            pltpu.VMEM((2, 2, PACK, H), F32),
            pltpu.VMEM((2, 2, W, W), F32),
            pltpu.VMEM((2, 2, PACK, H), F32),
            pltpu.VMEM((2, 2, PACK, H), F32),
            pltpu.VMEM((2, W, W), F32),
            pltpu.VMEM((2, ROWS, H), F32),
            pltpu.VMEM((2, 7, PART, H), F32),
            pltpu.VMEM((2, ROWS, H), F32),
            pltpu.VMEM((PACK, H), F32),
            dma((2,)),
            dma((2,)),
            dma((2, CHUNKS)),
            dma((2, CHUNKS)),
            dma((2, GROUP)),
            dma((2,)),
            dma((2, 7)),
            dma((2, 7)),
            dma((2, 7)),
            dma((2, 7)),
        ],
        compiler_params=pltpu.CompilerParams(
            collective_id=0, has_side_effects=True, vmem_limit_bytes=48 << 20
        ),
        name="selected_inversion",
    )(live_width_array, pole_weight, pivot_inverse, factor_block)


def solution(mesh):
    placed = (
        P("pole", "snode", None, None, None),
        P("pole", "snode", None, None, None),
        P("snode"),
        P("pole", None),
    )
    return jax.shard_map(
        functools.partial(local, mesh.shape["snode"]),
        mesh=mesh,
        in_specs=placed,
        out_specs=(P("snode", None, None), P("snode", None, None)),
        check_vma=False,
    )
```

```python
import functools

import jax
import jax.numpy as jnp
from jax import lax
from jax.experimental import pallas as pl
from jax.experimental.pallas import tpu as pltpu
from jax.sharding import PartitionSpec as P

MESH = pl.DeviceIdType.MESH
F32 = jnp.float32
BF = jnp.bfloat16
W = 256
H = 128
PACK = 264
PART = 104
ROWS = 8 * PART
GROUP = 4
OWN, GOT1, PAIR, GOT2, QUAD, GOT3, OCT = range(7)
NEAR = (1, 2, 4, 5, 7, 8)


def split(x):
    high = x.astype(BF)
    return high, (x - high.astype(F32)).astype(BF)


def csplit(pair):
    return split(pair[0]) + split(pair[1])


def dot(a, b):
    return jnp.dot(a, b, preferred_element_type=F32)


def dot_t(a, b):
    return lax.dot_general(a, b, (((0,), (0,)), ((), ())), preferred_element_type=F32)


def product(left, right, mul=dot):
    lrh, lrl, lih, lil = left
    rrh, rrl, rih, ril = right
    real = mul(lrh, rrh) - mul(lih, rih)
    real += (mul(lrl, rrh) + mul(lrh, rrl)) - (mul(lil, rih) + mul(lih, ril))
    imag = mul(lrh, rih) + mul(lih, rrh)
    imag += (mul(lrl, rih) + mul(lrh, ril)) + (mul(lil, rrh) + mul(lih, rrl))
    return real, imag


def sandwich(middle, outer):
    return product(outer, csplit(product(csplit(middle), outer)), dot_t)


def tri():
    row = lax.broadcasted_iota(jnp.int32, (H, H), 0)
    col = lax.broadcasted_iota(jnp.int32, (H, H), 1)
    return row, col


def pack_into(ref, block):
    row, col = tri()
    last = block[H:, H:]
    ref[0:H, :] = block[:H, H:]
    ref[H : 2 * H, :] = jnp.where(row <= col, block[:H, :H], last)
    diagonal = jnp.sum(jnp.where(row == col, last, 0.0), axis=0, keepdims=True)
    ref[2 * H : PACK, :] = jnp.broadcast_to(diagonal, (8, H))


def unpack(ref):
    row, col = tri()
    upper = ref[0:H, :]
    both = ref[H : 2 * H, :]
    both_t = both.T
    diagonal = ref[2 * H : 2 * H + 1, :]
    first = jnp.where(row <= col, both, both_t)
    last = jnp.where(row > col, both, jnp.where(row == col, diagonal, both_t))
    return jnp.concatenate(
        [jnp.concatenate([first, upper], 1), jnp.concatenate([upper.T, last], 1)], 0
    )


def unpack2(ref):
    return unpack(ref.at[0]), unpack(ref.at[1])


def pack2(ref, pair):
    pack_into(ref.at[0], pair[0])
    pack_into(ref.at[1], pair[1])


def kernel(
    nodes,
    width_hbm,
    weight_hbm,
    p_hbm,
    f_hbm,
    diag_ref,
    off_ref,
    p_ref,
    f_ref,
    width_ref,
    weight_ref,
    fs,
    steps_a,
    steps_b,
    got_a,
    got_b,
    out_a,
    out_b,
    jump,
    entry,
    head_out,
    pair_out,
    own_out,
    s_in,
    dens,
    parts,
    total,
    spare,
    load_sem,
    sent,
    got,
    rs_send,
    rs_recv,
    ag_send,
    ag_recv,
):
    me = lax.axis_index("pole")
    i = lax.axis_index("snode")
    groups = nodes // GROUP
    g = lax.rem(i, GROUP)
    m = lax.div(i, GROUP)
    low = 1 - lax.rem(m, 2)

    loads = [
        pltpu.make_async_copy(width_hbm, width_ref, load_sem.at[0]),
        pltpu.make_async_copy(weight_hbm, weight_ref, load_sem.at[1]),
    ]
    for p in range(2):
        loads.append(pltpu.make_async_copy(f_hbm.at[p], f_ref.at[p], load_sem.at[2 + 2 * p]))
        loads.append(pltpu.make_async_copy(p_hbm.at[p], p_ref.at[p], load_sem.at[3 + 2 * p]))
    for load in loads:
        load.start()

    barrier = pltpu.get_barrier_semaphore()
    for step in NEAR:
        for near in (lax.rem(i + step, nodes), lax.rem(i + nodes - step, nodes)):
            pl.semaphore_signal(barrier, inc=1, device_id=(me, near), device_id_type=MESH)
    for step in range(1, 8):
        pl.semaphore_signal(
            barrier, inc=1, device_id=(lax.rem(me + step, 8), i), device_id_type=MESH
        )

    row = lax.broadcasted_iota(jnp.int32, (W, W), 0)
    col = lax.broadcasted_iota(jnp.int32, (W, W), 1)

    def pivot(p, k):
        live = (row < width_ref[k]) & (col < width_ref[k])
        return tuple(jnp.where(live, p_ref[p, k, part], 0.0) for part in range(2))

    def load4(ref):
        return tuple(ref[n] for n in range(4))

    def store4(ref, four):
        for n in range(4):
            ref[n] = four[n]

    def both(body):
        def turn(n, carry):
            body(n)
            return carry

        lax.fori_loop(0, 2, turn, 0)

    def plus(p, low=low):
        return lax.rem(p + low, 2) == 1

    def first_sender(p):
        return lax.rem(g + lax.rem(p + low, 2), 2) == 1

    def second_sender(p):
        return (plus(p) & (g == 1)) | (~plus(p) & (g == 2))

    def head(p):
        return (plus(p) & (g == 3)) | (~plus(p) & (g == 0))

    composing = m > 0
    quads = composing & (m < groups - 1)
    lower = (low == 1) & quads & (m < groups - 2)
    upper = (low == 0) & quads & (m > 1)

    def remote(src, dst, p, kind, landing, to):
        return pltpu.make_async_remote_copy(
            src_ref=src,
            dst_ref=dst,
            send_sem=sent.at[p, kind],
            recv_sem=got.at[p, landing],
            device_id=(me, to),
            device_id_type=MESH,
        )

    def step_copies(p, level):
        out = jnp.int32(0) if level < 2 else jnp.int32(1)
        way = jnp.where(plus(p), 1, -1)
        if level == 2:
            to = jnp.where(plus(p), i + 1, i + 7)
        else:
            to = i + way * (level + 1)
        to = lax.rem(to + nodes, nodes)
        return [
            remote(out_a.at[p, out], got_a.at[p, level], p, 2 * (level // 2), 2 * level, to),
            remote(out_b.at[p, out], got_b.at[p, level], p, 2 * (level // 2) + 1, 2 * level + 1, to),
        ]

    def post_step(p, level, slot, a_pair):
        out = 0 if level < 2 else 1
        out_a[p, out, 0] = a_pair[0]
        out_a[p, out, 1] = a_pair[1]
        pack2(out_b.at[p, out], (steps_b[p, slot, 0], steps_b[p, slot, 1]))
        for copy in step_copies(p, level):
            copy.start()

    def head_copies(p, src):
        n = m + 1
        forward = lax.rem(p + 1 - lax.rem(n, 2), 2) == 1
        skip = (n == 2) | (n == 4)
        octs = (n == 3) | (n == 5)
        base = lax.rem(GROUP * n, nodes)
        after = lax.rem(GROUP * (n + 1) + 3 * p, nodes)
        real = n < groups
        return [
            (real & skip, remote(src.at[p], jump.at[p], p, 4, 6, after)),
            (real & forward & ~octs & (n < groups - 1), remote(src.at[p], jump.at[p], p, 5, 6, base + 3)),
            (real & forward, remote(src.at[p], jump.at[p], p, 6, 6, base + 1)),
            (real, remote(src.at[p], entry.at[p], p, 7, 7, base)),
        ]

    def send_head(p, src):
        for when, copy in head_copies(p, src):
            pl.when(when)(copy.start)

    def pair_copy(p, ahead):
        return remote(pair_out.at[p], entry.at[p], p, 8, 7, lax.rem(i + ahead, nodes))

    def own_copy(p):
        return remote(own_out.at[p], entry.at[p], p, 9, 7, lax.rem(i + 1, nodes))

    with jax.named_scope("own_steps"):
        loads[0].wait()
        for p in range(2):
            loads[2 + 2 * p].wait()
            for k in range(2):
                live = col < width_ref[k]
                store4(
                    fs.at[p, k],
                    csplit([jnp.where(live, f_ref[p, k, part], 0.0) for part in range(2)]),
                )
            real, imag = product(load4(fs.at[p, 0]), load4(fs.at[p, 1]))
            store4(steps_a.at[p, OWN], csplit((real, imag)))
            loads[3 + 2 * p].wait()
            inner = sandwich(pivot(p, 0), load4(fs.at[p, 1]))
            last = pivot(p, 1)
            for part in range(2):
                steps_b[p, OWN, part] = last[part] + inner[part]

            if p == 0:
                pl.semaphore_wait(barrier, 2 * len(NEAR) + 7)

            @pl.when(composing & first_sender(p))
            def _():
                post_step(p, 0, OWN, (real, imag))

    def merge(p, level, own, received, new, forward):
        for copy in step_copies(p, level):
            copy.wait_recv()
        store4(steps_a.at[p, received], csplit((got_a[p, level, 0], got_a[p, level, 1])))
        block = unpack2(got_b.at[p, level])
        steps_b[p, received, 0] = block[0]
        steps_b[p, received, 1] = block[1]
        first = jnp.where(forward, received, own)
        second = jnp.where(forward, own, received)
        outer = load4(steps_a.at[p, second])
        inner = sandwich((steps_b[p, first, 0], steps_b[p, first, 1]), outer)
        for part in range(2):
            steps_b[p, new, part] = steps_b[p, second, part] + inner[part]
        a_pair = product(load4(steps_a.at[p, first]), outer)
        store4(steps_a.at[p, new], csplit(a_pair))
        return a_pair

    with jax.named_scope("pairs"):

        @pl.when(composing)
        def _():
            def body(p):
                @pl.when(~first_sender(p))
                def _():
                    a_pair = merge(p, 0, OWN, GOT1, PAIR, plus(p))

                    @pl.when(quads & second_sender(p))
                    def _():
                        post_step(p, 1, PAIR, a_pair)

            both(body)

    with jax.named_scope("quads"):

        @pl.when(quads)
        def _():
            def body(p):
                @pl.when(head(p))
                def _():
                    a_pair = merge(p, 1, PAIR, GOT2, QUAD, plus(p))

                    @pl.when(lower)
                    def _():
                        post_step(p, 2, QUAD, a_pair)

            both(body)

    with jax.named_scope("octs"):

        @pl.when(upper)
        def _():
            def body(p):
                @pl.when(head(p))
                def _():
                    merge(p, 2, QUAD, GOT3, OCT, True)

            both(body)

    def advance(p, slot, state, ref):
        inner = sandwich(state, load4(steps_a.at[p, slot]))
        pack2(ref, (steps_b[p, slot, 0] + inner[0], steps_b[p, slot, 1] + inner[1]))

    def jumps(p):
        forward = plus(p) & ((g == 1) | ((g == 3) & quads))
        return composing & (forward | (upper & head(p)))

    with jax.named_scope("jumps"):

        def body(p):
            @pl.when(jumps(p))
            def _():
                remote(jump.at[p], jump.at[p], p, 4, 6, i).wait_recv()
                state = unpack2(jump.at[p])

                @pl.when(g == 1)
                def _():
                    advance(p, PAIR, state, pair_out.at[p])
                    pair_copy(p, 1).start()

                @pl.when(g != 1)
                def _():
                    advance(p, jnp.where(upper, OCT, QUAD), state, head_out.at[p])
                    send_head(p, head_out)

        both(body)

    def send_part(k, step):
        to = lax.rem(me + step, 8)
        return pltpu.make_async_remote_copy(
            src_ref=dens.at[k, pl.ds(pl.multiple_of(to * PART, 8), PART)],
            dst_ref=parts.at[k, step - 1],
            send_sem=rs_send.at[k, step - 1],
            recv_sem=rs_recv.at[k, step - 1],
            device_id=(to, i),
            device_id_type=MESH,
        )

    def send_total(k, step):
        to = lax.rem(me + step, 8)
        rows = pl.ds(pl.multiple_of(me * PART, 8), PART)
        return pltpu.make_async_remote_copy(
            src_ref=total.at[k, rows],
            dst_ref=total.at[k, rows],
            send_sem=ag_send.at[k, step - 1],
            recv_sem=ag_recv.at[k, step - 1],
            device_id=(to, i),
            device_id_type=MESH,
        )

    order = (4, 3, 5, 2, 6, 7, 1)

    def put(n, p, k, product_pair, inverse_pair):
        re_w, im_w = weight_ref[p, 0], weight_ref[p, 1]
        off = -(re_w * product_pair[1] + im_w * product_pair[0])
        diag = re_w * inverse_pair[1] + im_w * inverse_pair[0]
        mine = dens.at[k]
        if n == 0:
            mine[0:W, :] = off[:, :H]
            mine[W : 2 * W, :] = off[:, H:]
            pack_into(mine.at[pl.ds(2 * W, PACK)], diag)
            mine[2 * W + PACK : ROWS, :] = jnp.zeros((ROWS - 2 * W - PACK, H), F32)
        else:
            mine[0:W, :] += off[:, :H]
            mine[W : 2 * W, :] += off[:, H:]
            pack_into(spare, diag)
            mine[2 * W : 2 * W + PACK, :] += spare[...]
            for step in order:
                send_part(k, step).start()

    loads[1].wait()
    passes_on = (m == 0) | (lax.rem(g, 2) == 0)
    with jax.named_scope("states"):
        for n in range(2):
            p = lax.rem(low + n, 2)

            @pl.when(i == 0)
            def _():
                s_in[...] = jnp.zeros_like(s_in)

            @pl.when(i > 0)
            def _():
                remote(entry.at[p], entry.at[p], p, 7, 7, i).wait_recv()
                block = unpack2(entry.at[p])
                s_in[0] = block[0]
                s_in[1] = block[1]

            @pl.when(composing & (g == 0) & ~plus(p))
            def _():
                @pl.when(quads & ~upper)
                def _():
                    advance(p, QUAD, (s_in[0], s_in[1]), head_out.at[p])
                    send_head(p, head_out)

                advance(p, PAIR, (s_in[0], s_in[1]), pair_out.at[p])
                pair_copy(p, 2).start()

            @pl.when(passes_on)
            def _():
                advance(p, OWN, (s_in[0], s_in[1]), own_out.at[p])

                @pl.when((m > 0) | (g < 3))
                def _():
                    own_copy(p).start()

                @pl.when((m == 0) & (g == 3))
                def _():
                    send_head(p, own_out)

            state = (s_in[0], s_in[1])
            for k in range(2):
                link = load4(fs.at[p, k])
                moved = product(csplit(state), link)
                inner = product(link, csplit(moved), dot_t)
                block = pivot(p, k)
                state = (block[0] + inner[0], block[1] + inner[1])
                put(n, p, k, moved, state)

    with jax.named_scope("pole_sum"):
        mine = pl.ds(pl.multiple_of(me * PART, 8), PART)
        for k in range(2):
            acc = dens[k, mine]
            for step in range(1, 8):
                send_part(k, step).wait_recv()
                acc = acc + parts[k, step - 1]
            total[k, mine] = acc
            for step in order:
                send_total(k, step).start()
    with jax.named_scope("pole_gather"):
        for k in range(2):
            for step in range(1, 8):
                back = lax.rem(me + 8 - step, 8)
                rows = pl.ds(pl.multiple_of(back * PART, 8), PART)
                pltpu.make_async_remote_copy(
                    src_ref=total.at[k, rows],
                    dst_ref=total.at[k, rows],
                    send_sem=ag_send.at[k, step - 1],
                    recv_sem=ag_recv.at[k, step - 1],
                    device_id=(back, i),
                    device_id_type=MESH,
                ).wait_recv()
            off_ref[k, :, 0:H] = total[k, 0:W]
            off_ref[k, :, H:W] = total[k, W : 2 * W]
            diag_ref[k] = unpack(total.at[k, pl.ds(2 * W, PACK)])

    def body(p):
        @pl.when(composing & (first_sender(p) | (quads & second_sender(p))))
        def _():
            for copy in step_copies(p, 0):
                copy.wait_send()

        @pl.when(lower & head(p))
        def _():
            for copy in step_copies(p, 2):
                copy.wait_send()

        @pl.when((quads & head(p)) | ((m == 0) & (g == 3)))
        def _():
            for when, copy in head_copies(p, head_out):
                pl.when(when)(copy.wait_send)

        @pl.when(composing & ((plus(p) & (g == 1)) | (~plus(p) & (g == 0))))
        def _():
            pair_copy(p, 1).wait_send()

        @pl.when(passes_on & ((m > 0) | (g < 3)))
        def _():
            own_copy(p).wait_send()

    both(body)
    for k in range(2):
        for step in range(1, 8):
            send_part(k, step).wait_send()
            send_total(k, step).wait_send()


def local(nodes, pivot_inverse, factor_block, live_width_array, pole_weight):
    vmem = pl.BlockSpec(memory_space=pltpu.VMEM)
    hbm = pl.BlockSpec(memory_space=pl.ANY)
    dma = pltpu.SemaphoreType.DMA
    packed = pltpu.VMEM((2, 2, PACK, H), F32)
    return pl.pallas_call(
        functools.partial(kernel, nodes),
        out_shape=[jax.ShapeDtypeStruct((2, W, W), F32)] * 2,
        in_specs=[hbm, hbm, hbm, hbm],
        out_specs=[vmem, vmem],
        scratch_shapes=[
            pltpu.VMEM((2, 2, 2, W, W), F32),
            pltpu.VMEM((2, 2, 2, W, W), F32),
            pltpu.SMEM((2,), jnp.int32),
            pltpu.SMEM((2, 2), F32),
            pltpu.VMEM((2, 2, 4, W, W), BF),
            pltpu.VMEM((2, 7, 4, W, W), BF),
            pltpu.VMEM((2, 7, 2, W, W), F32),
            pltpu.VMEM((2, 3, 2, W, W), F32),
            pltpu.VMEM((2, 3, 2, PACK, H), F32),
            pltpu.VMEM((2, 2, 2, W, W), F32),
            pltpu.VMEM((2, 2, 2, PACK, H), F32),
            packed,
            packed,
            packed,
            packed,
            packed,
            pltpu.VMEM((2, W, W), F32),
            pltpu.VMEM((2, ROWS, H), F32),
            pltpu.VMEM((2, 7, PART, H), F32),
            pltpu.VMEM((2, ROWS, H), F32),
            pltpu.VMEM((PACK, H), F32),
            dma((6,)),
            dma((2, 10)),
            dma((2, 8)),
            dma((2, 7)),
            dma((2, 7)),
            dma((2, 7)),
            dma((2, 7)),
        ],
        compiler_params=pltpu.CompilerParams(
            collective_id=0, has_side_effects=True, vmem_limit_bytes=44 << 20
        ),
        name="selected_inversion",
    )(live_width_array, pole_weight, pivot_inverse, factor_block)


def solution(mesh):
    placed = (
        P("pole", "snode", None, None, None),
        P("pole", "snode", None, None, None),
        P("snode"),
        P("pole", None),
    )
    return jax.shard_map(
        functools.partial(local, mesh.shape["snode"]),
        mesh=mesh,
        in_specs=placed,
        out_specs=(P("snode", None, None), P("snode", None, None)),
        check_vma=False,
    )
```

```python
import functools

import jax
import jax.numpy as jnp
from jax import lax
from jax.experimental import pallas as pl
from jax.experimental.pallas import tpu as pltpu
from jax.sharding import PartitionSpec as P

MESH = pl.DeviceIdType.MESH
F32 = jnp.float32
BF = jnp.bfloat16
W = 256
H = 128
PACK = 264
PART = 104
ROWS = 8 * PART
GROUP = 4
VMEM_MIB = 52
OWN, GOT1, PAIR, GOT2, QUAD, GOT3, OCT = range(7)
NEAR = (1, 2, 4, 5, 7, 8)


def split(x):
    high = x.astype(BF)
    return high, (x - high.astype(F32)).astype(BF)


def csplit(pair):
    return split(pair[0]) + split(pair[1])


def dot(a, b):
    return jnp.dot(a, b, preferred_element_type=F32)


def dot_t(a, b):
    return lax.dot_general(a, b, (((0,), (0,)), ((), ())), preferred_element_type=F32)


def product(left, right, mul=dot):
    lrh, lrl, lih, lil = left
    rrh, rrl, rih, ril = right
    real = mul(lrh, rrh) - mul(lih, rih)
    real += (mul(lrl, rrh) + mul(lrh, rrl)) - (mul(lil, rih) + mul(lih, ril))
    imag = mul(lrh, rih) + mul(lih, rrh)
    imag += (mul(lrl, rih) + mul(lrh, ril)) + (mul(lil, rrh) + mul(lih, rrl))
    return real, imag


def sandwich(middle, outer):
    return product(outer, csplit(product(csplit(middle), outer)), dot_t)


def tri():
    row = lax.broadcasted_iota(jnp.int32, (H, H), 0)
    col = lax.broadcasted_iota(jnp.int32, (H, H), 1)
    return row, col


def pack_into(ref, block):
    row, col = tri()
    last = block[H:, H:]
    ref[0:H, :] = block[:H, H:]
    ref[H : 2 * H, :] = jnp.where(row <= col, block[:H, :H], last)
    diagonal = jnp.sum(jnp.where(row == col, last, 0.0), axis=0, keepdims=True)
    ref[2 * H : PACK, :] = jnp.broadcast_to(diagonal, (8, H))


def unpack(ref):
    row, col = tri()
    upper = ref[0:H, :]
    both = ref[H : 2 * H, :]
    both_t = both.T
    diagonal = ref[2 * H : 2 * H + 1, :]
    first = jnp.where(row <= col, both, both_t)
    last = jnp.where(row > col, both, jnp.where(row == col, diagonal, both_t))
    return jnp.concatenate(
        [jnp.concatenate([first, upper], 1), jnp.concatenate([upper.T, last], 1)], 0
    )


def unpack2(ref):
    return unpack(ref.at[0]), unpack(ref.at[1])


def pack2(ref, pair):
    pack_into(ref.at[0], pair[0])
    pack_into(ref.at[1], pair[1])


def kernel(
    nodes,
    width_hbm,
    weight_hbm,
    p_hbm,
    f_hbm,
    diag_ref,
    off_ref,
    p_ref,
    f_ref,
    width_ref,
    weight_ref,
    fs,
    steps_a,
    steps_b,
    got_a,
    got_b,
    out_a,
    out_b,
    jump,
    entry,
    head_out,
    pair_out,
    own_out,
    s_in,
    dens,
    parts,
    total,
    spare,
    load_sem,
    sent,
    got,
    rs_send,
    rs_recv,
    ag_send,
    ag_recv,
):
    me = lax.axis_index("pole")
    i = lax.axis_index("snode")
    groups = nodes // GROUP
    g = lax.rem(i, GROUP)
    m = lax.div(i, GROUP)
    low = 1 - lax.rem(m, 2)

    loads = [
        pltpu.make_async_copy(width_hbm, width_ref, load_sem.at[0]),
        pltpu.make_async_copy(weight_hbm, weight_ref, load_sem.at[1]),
    ]
    for p in range(2):
        loads.append(pltpu.make_async_copy(f_hbm.at[p], f_ref.at[p], load_sem.at[2 + 2 * p]))
        loads.append(pltpu.make_async_copy(p_hbm.at[p], p_ref.at[p], load_sem.at[3 + 2 * p]))
    for load in loads:
        load.start()

    barrier = pltpu.get_barrier_semaphore()
    for step in NEAR:
        for near in (lax.rem(i + step, nodes), lax.rem(i + nodes - step, nodes)):
            pl.semaphore_signal(barrier, inc=1, device_id=(me, near), device_id_type=MESH)
    for step in range(1, 8):
        pl.semaphore_signal(
            barrier, inc=1, device_id=(lax.rem(me + step, 8), i), device_id_type=MESH
        )

    row = lax.broadcasted_iota(jnp.int32, (W, W), 0)
    col = lax.broadcasted_iota(jnp.int32, (W, W), 1)

    def pivot(p, k):
        live = (row < width_ref[k]) & (col < width_ref[k])
        return tuple(jnp.where(live, p_ref[p, k, part], 0.0) for part in range(2))

    def load4(ref):
        return tuple(ref[n] for n in range(4))

    def store4(ref, four):
        for n in range(4):
            ref[n] = four[n]

    def both(body):
        def turn(n, carry):
            body(n)
            return carry

        lax.fori_loop(0, 2, turn, 0)

    def plus(p, low=low):
        return lax.rem(p + low, 2) == 1

    def first_sender(p):
        return lax.rem(g + lax.rem(p + low, 2), 2) == 1

    def second_sender(p):
        return (plus(p) & (g == 1)) | (~plus(p) & (g == 2))

    def head(p):
        return (plus(p) & (g == 3)) | (~plus(p) & (g == 0))

    composing = m > 0
    quads = composing & (m < groups - 1)
    lower = m == 4
    upper = m == 5

    def remote(src, dst, p, kind, landing, to):
        return pltpu.make_async_remote_copy(
            src_ref=src,
            dst_ref=dst,
            send_sem=sent.at[p, kind],
            recv_sem=got.at[p, landing],
            device_id=(me, to),
            device_id_type=MESH,
        )

    def step_copies(p, level):
        out = jnp.int32(0) if level < 2 else jnp.int32(1)
        way = jnp.where(plus(p), 1, -1)
        if level == 2:
            to = jnp.where(plus(p), i + 1, i + 7)
        else:
            to = i + way * (level + 1)
        to = lax.rem(to + nodes, nodes)
        return [
            remote(out_a.at[p, out], got_a.at[p, level], p, 2 * (level // 2), 2 * level, to),
            remote(out_b.at[p, out], got_b.at[p, level], p, 2 * (level // 2) + 1, 2 * level + 1, to),
        ]

    def post_step(p, level, slot, a_pair):
        out = 0 if level < 2 else 1
        out_a[p, out, 0] = a_pair[0]
        out_a[p, out, 1] = a_pair[1]
        pack2(out_b.at[p, out], (steps_b[p, slot, 0], steps_b[p, slot, 1]))
        for copy in step_copies(p, level):
            copy.start()

    def head_copies(p, src):
        n = m + 1
        forward = lax.rem(p + 1 - lax.rem(n, 2), 2) == 1
        base = lax.rem(GROUP * n, nodes)
        after = lax.rem(GROUP * (n + 1) + 3 * p, nodes)
        to_oct = n == 4
        to_head = forward & (n != 5) & (n < groups - 1)
        to_pair = forward & (n < groups)
        to_base = n < groups
        oct_copy = remote(src.at[p], jump.at[p], p, 4, 6, after)
        head_copy = remote(src.at[p], jump.at[p], p, 5, 6, base + 3)
        pair = remote(src.at[p], jump.at[p], p, 6, 6, base + 1)
        base_copy = remote(src.at[p], entry.at[p], p, 7, 7, base)
        urgent = [
            (to_oct, oct_copy),
            (to_head & ~to_oct, head_copy),
            (to_pair & ~to_head & ~to_oct, pair),
            (to_base & ~to_pair & ~to_oct, base_copy),
        ]
        rest = [
            (to_head & to_oct, head_copy),
            (to_pair & (to_head | to_oct), pair),
            (to_base & (to_pair | to_oct), base_copy),
        ]
        return urgent, rest

    def send_head(p, src):
        for when, copy in head_copies(p, src)[0]:
            pl.when(when)(copy.start)

    def send_rest(p, src):
        urgent, rest = head_copies(p, src)
        for when, copy in urgent:
            pl.when(when)(copy.wait_send)
        for when, copy in rest:
            pl.when(when)(copy.start)

    def pair_copy(p, ahead):
        return remote(pair_out.at[p], entry.at[p], p, 8, 7, lax.rem(i + ahead, nodes))

    def own_copy(p):
        return remote(own_out.at[p], entry.at[p], p, 9, 7, lax.rem(i + 1, nodes))

    with jax.named_scope("own_steps"):
        loads[0].wait()
        for p in range(2):
            loads[2 + 2 * p].wait()
            for k in range(2):
                live = col < width_ref[k]
                store4(
                    fs.at[p, k],
                    csplit([jnp.where(live, f_ref[p, k, part], 0.0) for part in range(2)]),
                )
            real, imag = product(load4(fs.at[p, 0]), load4(fs.at[p, 1]))
            store4(steps_a.at[p, OWN], csplit((real, imag)))
            loads[3 + 2 * p].wait()
            inner = sandwich(pivot(p, 0), load4(fs.at[p, 1]))
            last = pivot(p, 1)
            for part in range(2):
                steps_b[p, OWN, part] = last[part] + inner[part]

            if p == 0:
                pl.semaphore_wait(barrier, 2 * len(NEAR) + 7)

            @pl.when(composing & first_sender(p))
            def _():
                post_step(p, 0, OWN, (real, imag))

    def merge(p, level, own, received, new, forward):
        for copy in step_copies(p, level):
            copy.wait_recv()
        store4(steps_a.at[p, received], csplit((got_a[p, level, 0], got_a[p, level, 1])))
        block = unpack2(got_b.at[p, level])
        steps_b[p, received, 0] = block[0]
        steps_b[p, received, 1] = block[1]
        first = jnp.where(forward, received, own)
        second = jnp.where(forward, own, received)
        outer = load4(steps_a.at[p, second])
        inner = sandwich((steps_b[p, first, 0], steps_b[p, first, 1]), outer)
        for part in range(2):
            steps_b[p, new, part] = steps_b[p, second, part] + inner[part]
        a_pair = product(load4(steps_a.at[p, first]), outer)
        store4(steps_a.at[p, new], csplit(a_pair))
        return a_pair

    with jax.named_scope("pairs"):

        @pl.when(composing)
        def _():
            def body(p):
                @pl.when(~first_sender(p))
                def _():
                    a_pair = merge(p, 0, OWN, GOT1, PAIR, plus(p))

                    @pl.when(quads & second_sender(p))
                    def _():
                        post_step(p, 1, PAIR, a_pair)

            both(body)

    with jax.named_scope("quads"):

        @pl.when(quads)
        def _():
            def body(p):
                @pl.when(head(p))
                def _():
                    a_pair = merge(p, 1, PAIR, GOT2, QUAD, plus(p))

                    @pl.when(lower)
                    def _():
                        post_step(p, 2, QUAD, a_pair)

            both(body)

    with jax.named_scope("octs"):

        @pl.when(upper)
        def _():
            def body(p):
                @pl.when(head(p))
                def _():
                    merge(p, 2, QUAD, GOT3, OCT, True)

            both(body)

    def advance(p, slot, state, ref):
        inner = sandwich(state, load4(steps_a.at[p, slot]))
        pack2(ref, (steps_b[p, slot, 0] + inner[0], steps_b[p, slot, 1] + inner[1]))

    def jumps(p):
        forward = plus(p) & ((g == 1) | ((g == 3) & quads))
        return composing & (forward | (upper & head(p)))

    with jax.named_scope("jumps"):

        def body(p):
            @pl.when(jumps(p))
            def _():
                remote(jump.at[p], jump.at[p], p, 4, 6, i).wait_recv()
                state = unpack2(jump.at[p])

                @pl.when(g == 1)
                def _():
                    advance(p, PAIR, state, pair_out.at[p])
                    pair_copy(p, 1).start()

                @pl.when(g != 1)
                def _():
                    advance(p, jnp.where(upper, OCT, QUAD), state, head_out.at[p])
                    send_head(p, head_out)
                    send_rest(p, head_out)

        both(body)

    def send_part(k, step):
        to = lax.rem(me + step, 8)
        return pltpu.make_async_remote_copy(
            src_ref=dens.at[k, pl.ds(pl.multiple_of(to * PART, 8), PART)],
            dst_ref=parts.at[k, step - 1],
            send_sem=rs_send.at[k, step - 1],
            recv_sem=rs_recv.at[k, step - 1],
            device_id=(to, i),
            device_id_type=MESH,
        )

    def send_total(k, step):
        to = lax.rem(me + step, 8)
        rows = pl.ds(pl.multiple_of(me * PART, 8), PART)
        return pltpu.make_async_remote_copy(
            src_ref=total.at[k, rows],
            dst_ref=total.at[k, rows],
            send_sem=ag_send.at[k, step - 1],
            recv_sem=ag_recv.at[k, step - 1],
            device_id=(to, i),
            device_id_type=MESH,
        )

    order = (4, 3, 5, 2, 6, 7, 1)

    def put(n, p, k, product_pair, inverse_pair):
        re_w, im_w = weight_ref[p, 0], weight_ref[p, 1]
        off = -(re_w * product_pair[1] + im_w * product_pair[0])
        diag = re_w * inverse_pair[1] + im_w * inverse_pair[0]
        mine = dens.at[k]
        if n == 0:
            mine[0:W, :] = off[:, :H]
            mine[W : 2 * W, :] = off[:, H:]
            pack_into(mine.at[pl.ds(2 * W, PACK)], diag)
            mine[2 * W + PACK : ROWS, :] = jnp.zeros((ROWS - 2 * W - PACK, H), F32)
        else:
            mine[0:W, :] += off[:, :H]
            mine[W : 2 * W, :] += off[:, H:]
            pack_into(spare, diag)
            mine[2 * W : 2 * W + PACK, :] += spare[...]
            for step in order:
                send_part(k, step).start()

    loads[1].wait()
    passes_on = (m == 0) | (lax.rem(g, 2) == 0)

    def enter(p):
        @pl.when(i == 0)
        def _():
            s_in[p] = jnp.zeros_like(s_in[p])
            pack2(own_out.at[p], (steps_b[p, OWN, 0], steps_b[p, OWN, 1]))
            own_copy(p).start()

        @pl.when(i > 0)
        def _():
            remote(entry.at[p], entry.at[p], p, 7, 7, i).wait_recv()
            block = unpack2(entry.at[p])
            s_in[p, 0] = block[0]
            s_in[p, 1] = block[1]

        @pl.when(composing & (g == 0) & ~plus(p))
        def _():
            @pl.when(quads & ~upper)
            def _():
                advance(p, QUAD, (s_in[p, 0], s_in[p, 1]), head_out.at[p])
                send_head(p, head_out)

            advance(p, PAIR, (s_in[p, 0], s_in[p, 1]), pair_out.at[p])
            pair_copy(p, 2).start()

        @pl.when(passes_on & (i > 0))
        def _():
            advance(p, OWN, (s_in[p, 0], s_in[p, 1]), own_out.at[p])

            @pl.when((m > 0) | (g < 3))
            def _():
                own_copy(p).start()

            @pl.when((m == 0) & (g == 3))
            def _():
                send_head(p, own_out)
                send_rest(p, own_out)

        @pl.when(quads & ~upper & (g == 0) & ~plus(p))
        def _():
            send_rest(p, head_out)

    def details(n, p):
        state = (s_in[p, 0], s_in[p, 1])
        for k in range(2):
            link = load4(fs.at[p, k])
            moved = product(csplit(state), link)
            inner = product(link, csplit(moved), dot_t)
            block = pivot(p, k)
            state = (block[0] + inner[0], block[1] + inner[1])
            put(n, p, k, moved, state)

    with jax.named_scope("states"):
        one, two = lax.rem(low, 2), lax.rem(low + 1, 2)
        enter(one)

        @pl.when(~passes_on)
        def _():
            details(0, one)

        enter(two)

        @pl.when(passes_on)
        def _():
            details(0, one)

    with jax.named_scope("last_details"):
        details(1, two)

    with jax.named_scope("pole_sum"):
        mine = pl.ds(pl.multiple_of(me * PART, 8), PART)
        for k in range(2):
            acc = dens[k, mine]
            for step in range(1, 8):
                send_part(k, step).wait_recv()
                acc = acc + parts[k, step - 1]
            total[k, mine] = acc
            for step in order:
                send_total(k, step).start()
    with jax.named_scope("pole_gather"):
        for k in range(2):
            for step in range(1, 8):
                back = lax.rem(me + 8 - step, 8)
                rows = pl.ds(pl.multiple_of(back * PART, 8), PART)
                pltpu.make_async_remote_copy(
                    src_ref=total.at[k, rows],
                    dst_ref=total.at[k, rows],
                    send_sem=ag_send.at[k, step - 1],
                    recv_sem=ag_recv.at[k, step - 1],
                    device_id=(back, i),
                    device_id_type=MESH,
                ).wait_recv()
            off_ref[k, :, 0:H] = total[k, 0:W]
            off_ref[k, :, H:W] = total[k, W : 2 * W]
            diag_ref[k] = unpack(total.at[k, pl.ds(2 * W, PACK)])

    def body(p):
        @pl.when(composing & (first_sender(p) | (quads & second_sender(p))))
        def _():
            for copy in step_copies(p, 0):
                copy.wait_send()

        @pl.when(lower & head(p))
        def _():
            for copy in step_copies(p, 2):
                copy.wait_send()

        @pl.when((quads & head(p)) | ((m == 0) & (g == 3)))
        def _():
            for when, copy in head_copies(p, head_out)[1]:
                pl.when(when)(copy.wait_send)

        @pl.when(composing & ((plus(p) & (g == 1)) | (~plus(p) & (g == 0))))
        def _():
            pair_copy(p, 1).wait_send()

        @pl.when(passes_on & ((m > 0) | (g < 3)))
        def _():
            own_copy(p).wait_send()

    both(body)
    for k in range(2):
        for step in range(1, 8):
            send_part(k, step).wait_send()
            send_total(k, step).wait_send()


def local(nodes, pivot_inverse, factor_block, live_width_array, pole_weight):
    vmem = pl.BlockSpec(memory_space=pltpu.VMEM)
    hbm = pl.BlockSpec(memory_space=pl.ANY)
    dma = pltpu.SemaphoreType.DMA
    packed = pltpu.VMEM((2, 2, PACK, H), F32)
    return pl.pallas_call(
        functools.partial(kernel, nodes),
        out_shape=[jax.ShapeDtypeStruct((2, W, W), F32)] * 2,
        in_specs=[hbm, hbm, hbm, hbm],
        out_specs=[vmem, vmem],
        scratch_shapes=[
            pltpu.VMEM((2, 2, 2, W, W), F32),
            pltpu.VMEM((2, 2, 2, W, W), F32),
            pltpu.SMEM((2,), jnp.int32),
            pltpu.SMEM((2, 2), F32),
            pltpu.VMEM((2, 2, 4, W, W), BF),
            pltpu.VMEM((2, 7, 4, W, W), BF),
            pltpu.VMEM((2, 7, 2, W, W), F32),
            pltpu.VMEM((2, 3, 2, W, W), F32),
            pltpu.VMEM((2, 3, 2, PACK, H), F32),
            pltpu.VMEM((2, 2, 2, W, W), F32),
            pltpu.VMEM((2, 2, 2, PACK, H), F32),
            packed,
            packed,
            packed,
            packed,
            packed,
            pltpu.VMEM((2, 2, W, W), F32),
            pltpu.VMEM((2, ROWS, H), F32),
            pltpu.VMEM((2, 7, PART, H), F32),
            pltpu.VMEM((2, ROWS, H), F32),
            pltpu.VMEM((PACK, H), F32),
            dma((6,)),
            dma((2, 10)),
            dma((2, 8)),
            dma((2, 7)),
            dma((2, 7)),
            dma((2, 7)),
            dma((2, 7)),
        ],
        compiler_params=pltpu.CompilerParams(
            collective_id=0, has_side_effects=True, vmem_limit_bytes=VMEM_MIB << 20
        ),
        name="selected_inversion",
    )(live_width_array, pole_weight, pivot_inverse, factor_block)


def solution(mesh):
    placed = (
        P("pole", "snode", None, None, None),
        P("pole", "snode", None, None, None),
        P("snode"),
        P("pole", None),
    )
    return jax.shard_map(
        functools.partial(local, mesh.shape["snode"]),
        mesh=mesh,
        in_specs=placed,
        out_specs=(P("snode", None, None), P("snode", None, None)),
        check_vma=False,
    )
```

```python
import functools

import jax
import jax.numpy as jnp
from jax import lax
from jax.experimental import pallas as pl
from jax.experimental.pallas import tpu as pltpu
from jax.sharding import PartitionSpec as P

MESH = pl.DeviceIdType.MESH
F32 = jnp.float32
BF = jnp.bfloat16
W = 256
H = 128
PACK = 264
PART = 104
ROWS = 8 * PART
GROUP = 4
VMEM_MIB = 52
OWN, GOT1, PAIR, GOT2, QUAD, GOT3, OCT = range(7)
NEAR = (1, 2, 4, 5, 7, 8)


def split(x):
    high = x.astype(BF)
    return high, (x - high.astype(F32)).astype(BF)


def csplit(pair):
    return split(pair[0]) + split(pair[1])


def dot(a, b):
    return jnp.dot(a, b, preferred_element_type=F32)


def dot_t(a, b):
    return lax.dot_general(a, b, (((0,), (0,)), ((), ())), preferred_element_type=F32)


def product(left, right, mul=dot):
    lrh, lrl, lih, lil = left
    rrh, rrl, rih, ril = right
    real = mul(lrh, rrh) - mul(lih, rih)
    real += (mul(lrl, rrh) + mul(lrh, rrl)) - (mul(lil, rih) + mul(lih, ril))
    imag = mul(lrh, rih) + mul(lih, rrh)
    imag += (mul(lrl, rih) + mul(lrh, ril)) + (mul(lil, rrh) + mul(lih, rrl))
    return real, imag


def sandwich(middle, outer):
    return product(outer, csplit(product(csplit(middle), outer)), dot_t)


def tri():
    row = lax.broadcasted_iota(jnp.int32, (H, H), 0)
    col = lax.broadcasted_iota(jnp.int32, (H, H), 1)
    return row, col


def pack_into(ref, block):
    row, col = tri()
    last = block[H:, H:]
    ref[0:H, :] = block[:H, H:]
    ref[H : 2 * H, :] = jnp.where(row <= col, block[:H, :H], last)
    diagonal = jnp.sum(jnp.where(row == col, last, 0.0), axis=0, keepdims=True)
    ref[2 * H : PACK, :] = jnp.broadcast_to(diagonal, (8, H))


def unpack(ref):
    row, col = tri()
    upper = ref[0:H, :]
    both = ref[H : 2 * H, :]
    both_t = both.T
    diagonal = ref[2 * H : 2 * H + 1, :]
    first = jnp.where(row <= col, both, both_t)
    last = jnp.where(row > col, both, jnp.where(row == col, diagonal, both_t))
    return jnp.concatenate(
        [jnp.concatenate([first, upper], 1), jnp.concatenate([upper.T, last], 1)], 0
    )


def unpack2(ref):
    return unpack(ref.at[0]), unpack(ref.at[1])


def pack2(ref, pair):
    pack_into(ref.at[0], pair[0])
    pack_into(ref.at[1], pair[1])


def kernel(
    nodes,
    width_hbm,
    weight_hbm,
    p_hbm,
    f_hbm,
    diag_ref,
    off_ref,
    p_ref,
    f_ref,
    width_ref,
    weight_ref,
    fs,
    steps_a,
    steps_b,
    got_a,
    got_b,
    out_a,
    out_b,
    jump,
    entry,
    head_out,
    pair_out,
    own_out,
    s_in,
    dens,
    parts,
    total,
    spare,
    load_sem,
    sent,
    got,
    rs_send,
    rs_recv,
    ag_send,
    ag_recv,
):
    me = lax.axis_index("pole")
    i = lax.axis_index("snode")
    groups = nodes // GROUP
    g = lax.rem(i, GROUP)
    m = lax.div(i, GROUP)
    low = 1 - lax.rem(m, 2)

    loads = [
        pltpu.make_async_copy(width_hbm, width_ref, load_sem.at[0]),
        pltpu.make_async_copy(weight_hbm, weight_ref, load_sem.at[1]),
    ]
    for p in range(2):
        loads.append(pltpu.make_async_copy(f_hbm.at[p], f_ref.at[p], load_sem.at[2 + 2 * p]))
        loads.append(pltpu.make_async_copy(p_hbm.at[p], p_ref.at[p], load_sem.at[3 + 2 * p]))
    for load in loads:
        load.start()

    barrier = pltpu.get_barrier_semaphore()
    for step in NEAR:
        for near in (lax.rem(i + step, nodes), lax.rem(i + nodes - step, nodes)):
            pl.semaphore_signal(barrier, inc=1, device_id=(me, near), device_id_type=MESH)
    for step in range(1, 8):
        pl.semaphore_signal(
            barrier, inc=1, device_id=(lax.rem(me + step, 8), i), device_id_type=MESH
        )

    row = lax.broadcasted_iota(jnp.int32, (W, W), 0)
    col = lax.broadcasted_iota(jnp.int32, (W, W), 1)

    def pivot(p, k):
        live = (row < width_ref[k]) & (col < width_ref[k])
        return tuple(jnp.where(live, p_ref[p, k, part], 0.0) for part in range(2))

    def load4(ref):
        return tuple(ref[n] for n in range(4))

    def store4(ref, four):
        for n in range(4):
            ref[n] = four[n]

    def both(body):
        def turn(n, carry):
            body(n)
            return carry

        lax.fori_loop(0, 2, turn, 0)

    def plus(p, low=low):
        return lax.rem(p + low, 2) == 1

    def first_sender(p):
        return lax.rem(g + lax.rem(p + low, 2), 2) == 1

    def second_sender(p):
        return (plus(p) & (g == 1)) | (~plus(p) & (g == 2))

    def head(p):
        return (plus(p) & (g == 3)) | (~plus(p) & (g == 0))

    composing = m > 0
    quads = composing & (m < groups - 1)
    lower = m == 4
    upper = m == 5

    def remote(src, dst, p, kind, landing, to):
        return pltpu.make_async_remote_copy(
            src_ref=src,
            dst_ref=dst,
            send_sem=sent.at[p, kind],
            recv_sem=got.at[p, landing],
            device_id=(me, to),
            device_id_type=MESH,
        )

    def step_copies(p, level):
        out = jnp.int32(0) if level < 2 else jnp.int32(1)
        way = jnp.where(plus(p), 1, -1)
        if level == 2:
            to = jnp.where(plus(p), i + 1, i + 7)
        else:
            to = i + way * (level + 1)
        to = lax.rem(to + nodes, nodes)
        return [
            remote(out_a.at[p, out], got_a.at[p, level], p, 2 * (level // 2), 2 * level, to),
            remote(out_b.at[p, out], got_b.at[p, level], p, 2 * (level // 2) + 1, 2 * level + 1, to),
        ]

    def post_a(p, level, a_pair):
        out = 0 if level < 2 else 1
        out_a[p, out, 0] = a_pair[0]
        out_a[p, out, 1] = a_pair[1]

    def post_b(p, level, slot):
        out = 0 if level < 2 else 1
        pack2(out_b.at[p, out], (steps_b[p, slot, 0], steps_b[p, slot, 1]))

    def head_copies(p, src):
        n = m + 1
        forward = lax.rem(p + 1 - lax.rem(n, 2), 2) == 1
        base = GROUP * n
        ahead = jnp.where(
            n == 4, base + 4 + 3 * p, base + jnp.where((n == 5) | (n == groups - 1), 1, 3)
        )
        to_jump = (n < groups) & (forward | (n == 4))
        to_entry = (n < groups) & ~to_jump
        return [
            (to_jump, remote(src.at[p], jump.at[p], p, 4, 6, lax.rem(ahead, nodes))),
            (to_entry, remote(src.at[p], entry.at[p], p, 4, 7, lax.rem(base, nodes))),
            ((n == 4) & forward, remote(src.at[p], jump.at[p], p, 6, 6, lax.rem(base + 3, nodes))),
            ((n == 4) & ~forward, remote(src.at[p], entry.at[p], p, 6, 7, lax.rem(base, nodes))),
        ]

    def send_head(p, src):
        for when, copy in head_copies(p, src):
            pl.when(when)(copy.start)

    def relay_copies(p):
        to_jump = quads & ~upper & plus(p) & (g == 3)
        to_entry = composing & plus(p) & (g == 1)
        return [
            (to_jump, remote(jump.at[p], jump.at[p], p, 5, 6, lax.rem(i + nodes - 2, nodes))),
            (to_entry, remote(jump.at[p], entry.at[p], p, 5, 7, lax.rem(i + nodes - 1, nodes))),
        ]

    def pair_copy(p, ahead):
        return remote(pair_out.at[p], entry.at[p], p, 8, 7, lax.rem(i + ahead, nodes))

    def own_copy(p):
        return remote(own_out.at[p], entry.at[p], p, 9, 7, lax.rem(i + 1, nodes))

    with jax.named_scope("own_steps"):
        loads[0].wait()
        for p in range(2):
            loads[2 + 2 * p].wait()
            for k in range(2):
                live = col < width_ref[k]
                store4(
                    fs.at[p, k],
                    csplit([jnp.where(live, f_ref[p, k, part], 0.0) for part in range(2)]),
                )
            real, imag = product(load4(fs.at[p, 0]), load4(fs.at[p, 1]))
            store4(steps_a.at[p, OWN], csplit((real, imag)))

            if p == 0:

                @pl.when(low == 0)
                def _():
                    pl.semaphore_wait(barrier, 2 * len(NEAR) + 7)

            @pl.when(composing & first_sender(p))
            def _():
                post_a(p, 0, (real, imag))

                @pl.when(low == 0)
                def _():
                    step_copies(p, 0)[0].start()

        for p in range(2):
            loads[3 + 2 * p].wait()
            inner = sandwich(pivot(p, 0), load4(fs.at[p, 1]))
            last = pivot(p, 1)
            for part in range(2):
                steps_b[p, OWN, part] = last[part] + inner[part]

            @pl.when(composing & first_sender(p))
            def _():
                post_b(p, 0, OWN)

                @pl.when(low == 0)
                def _():
                    step_copies(p, 0)[1].start()

        @pl.when(low == 1)
        def _():
            pl.semaphore_wait(barrier, 2 * len(NEAR) + 7)
            for p in range(2):

                @pl.when(composing & first_sender(p))
                def _():
                    for copy in step_copies(p, 0):
                        copy.start()


    def merge(p, level, own, received, new, forward, sends):
        copies = step_copies(p, level)
        copies[0].wait_recv()
        store4(steps_a.at[p, received], csplit((got_a[p, level, 0], got_a[p, level, 1])))
        first = jnp.where(forward, received, own)
        second = jnp.where(forward, own, received)
        a_pair = product(load4(steps_a.at[p, first]), load4(steps_a.at[p, second]))
        store4(steps_a.at[p, new], csplit(a_pair))
        if sends is not None:

            @pl.when(sends)
            def _():
                post_a(p, level + 1, a_pair)
                step_copies(p, level + 1)[0].start()

        copies[1].wait_recv()
        block = unpack2(got_b.at[p, level])
        steps_b[p, received, 0] = block[0]
        steps_b[p, received, 1] = block[1]
        inner = sandwich((steps_b[p, first, 0], steps_b[p, first, 1]), load4(steps_a.at[p, second]))
        for part in range(2):
            steps_b[p, new, part] = steps_b[p, second, part] + inner[part]
        if sends is not None:

            @pl.when(sends)
            def _():
                post_b(p, level + 1, new)
                step_copies(p, level + 1)[1].start()

    with jax.named_scope("pairs"):

        @pl.when(composing)
        def _():
            def body(p):
                @pl.when(~first_sender(p))
                def _():
                    merge(p, 0, OWN, GOT1, PAIR, plus(p), quads & second_sender(p))

            both(body)

    with jax.named_scope("quads"):

        @pl.when(quads)
        def _():
            def body(p):
                @pl.when(head(p))
                def _():
                    merge(p, 1, PAIR, GOT2, QUAD, plus(p), lower)

            both(body)

    with jax.named_scope("octs"):

        @pl.when(upper)
        def _():
            def body(p):
                @pl.when(head(p))
                def _():
                    merge(p, 2, QUAD, GOT3, OCT, True, None)

            both(body)

    def advance(p, slot, state, ref):
        inner = sandwich(state, load4(steps_a.at[p, slot]))
        pack2(ref, (steps_b[p, slot, 0] + inner[0], steps_b[p, slot, 1] + inner[1]))

    def jumps(p):
        forward = plus(p) & ((g == 1) | ((g == 3) & quads))
        return composing & (forward | (upper & head(p)))

    with jax.named_scope("jumps"):

        def body(p):
            @pl.when(jumps(p))
            def _():
                remote(jump.at[p], jump.at[p], p, 4, 6, i).wait_recv()
                for when, copy in relay_copies(p):
                    pl.when(when)(copy.start)
                state = unpack2(jump.at[p])

                @pl.when(g == 1)
                def _():
                    advance(p, PAIR, state, pair_out.at[p])
                    pair_copy(p, 1).start()

                @pl.when(g != 1)
                def _():
                    advance(p, jnp.where(upper, OCT, QUAD), state, head_out.at[p])
                    send_head(p, head_out)

        both(body)

    def send_part(k, step):
        to = lax.rem(me + step, 8)
        return pltpu.make_async_remote_copy(
            src_ref=dens.at[k, pl.ds(pl.multiple_of(to * PART, 8), PART)],
            dst_ref=parts.at[k, step - 1],
            send_sem=rs_send.at[k, step - 1],
            recv_sem=rs_recv.at[k, step - 1],
            device_id=(to, i),
            device_id_type=MESH,
        )

    sibling = me + 1 - 2 * lax.rem(me, 2)

    def send_total(k, owner, to, slot):
        rows = pl.ds(pl.multiple_of(owner * PART, 8), PART)
        return pltpu.make_async_remote_copy(
            src_ref=total.at[k, rows],
            dst_ref=total.at[k, rows],
            send_sem=ag_send.at[k, slot],
            recv_sem=ag_recv.at[k, slot],
            device_id=(to, i),
            device_id_type=MESH,
        )

    def same_core(step):
        return lax.rem(me + step, 8)

    def first_totals(k):
        copies = [send_total(k, me, same_core(step), step - 1) for step in (4, 2, 6)]
        return copies + [send_total(k, me, sibling, 0)]

    order = (4, 3, 5, 2, 6, 7, 1)

    def put(n, p, k, product_pair, inverse_pair):
        re_w, im_w = weight_ref[p, 0], weight_ref[p, 1]
        off = -(re_w * product_pair[1] + im_w * product_pair[0])
        diag = re_w * inverse_pair[1] + im_w * inverse_pair[0]
        mine = dens.at[k]
        if n == 0:
            mine[0:W, :] = off[:, :H]
            mine[W : 2 * W, :] = off[:, H:]
            pack_into(mine.at[pl.ds(2 * W, PACK)], diag)
            mine[2 * W + PACK : ROWS, :] = jnp.zeros((ROWS - 2 * W - PACK, H), F32)
        else:
            mine[0:W, :] += off[:, :H]
            mine[W : 2 * W, :] += off[:, H:]
            pack_into(spare, diag)
            mine[2 * W : 2 * W + PACK, :] += spare[...]
            for step in order:
                send_part(k, step).start()

    loads[1].wait()
    passes_on = (m == 0) | (lax.rem(g, 2) == 0)

    later = composing & (g == 0)

    def enter(p, hold):
        @pl.when(i == 0)
        def _():
            s_in[p] = jnp.zeros_like(s_in[p])
            pack2(own_out.at[p], (steps_b[p, OWN, 0], steps_b[p, OWN, 1]))
            own_copy(p).start()

        @pl.when(i > 0)
        def _():
            remote(entry.at[p], entry.at[p], p, 7, 7, i).wait_recv()
            block = unpack2(entry.at[p])
            s_in[p, 0] = block[0]
            s_in[p, 1] = block[1]

        @pl.when(composing & (g == 0) & ~plus(p))
        def _():
            @pl.when(quads & ~upper)
            def _():
                advance(p, QUAD, (s_in[p, 0], s_in[p, 1]), head_out.at[p])
                send_head(p, head_out)

            advance(p, PAIR, (s_in[p, 0], s_in[p, 1]), pair_out.at[p])
            pair_copy(p, 2).start()

        @pl.when(passes_on & (i > 0))
        def _():
            advance(p, OWN, (s_in[p, 0], s_in[p, 1]), own_out.at[p])

            @pl.when(((m > 0) | (g < 3)) & ~(later & hold))
            def _():
                own_copy(p).start()

            @pl.when((m == 0) & (g == 3))
            def _():
                send_head(p, own_out)

    def details(n, p):
        state = (s_in[p, 0], s_in[p, 1])
        for k in range(2):
            link = load4(fs.at[p, k])
            moved = product(csplit(state), link)
            inner = product(link, csplit(moved), dot_t)
            block = pivot(p, k)
            state = (block[0] + inner[0], block[1] + inner[1])
            put(n, p, k, moved, state)

    with jax.named_scope("states"):
        one, two = lax.rem(low, 2), lax.rem(low + 1, 2)
        enter(one, True)

        @pl.when(~passes_on | later)
        def _():
            details(0, one)

            @pl.when(later)
            def _():
                own_copy(one).start()

        enter(two, False)

        @pl.when(passes_on & ~later)
        def _():
            details(0, one)

    with jax.named_scope("last_details"):
        details(1, two)

    with jax.named_scope("pole_sum"):
        mine = pl.ds(pl.multiple_of(me * PART, 8), PART)
        for k in range(2):
            acc = dens[k, mine]
            for step in range(1, 8):
                send_part(k, step).wait_recv()
                acc = acc + parts[k, step - 1]
            total[k, mine] = acc
            for copy in first_totals(k):
                copy.start()
    with jax.named_scope("pole_gather"):
        def pass_on(k, step):
            return send_total(k, lax.rem(me + 8 - step, 8), sibling, step)

        for k in range(2):
            for step in (2, 6, 4):
                send_total(k, lax.rem(me + 8 - step, 8), me, step - 1).wait_recv()
                pass_on(k, step).start()
        for k in range(2):
            send_total(k, sibling, me, 0).wait_recv()
            for step in (2, 6, 4):
                send_total(k, lax.rem(sibling + 8 - step, 8), me, step).wait_recv()
            off_ref[k, :, 0:H] = total[k, 0:W]
            off_ref[k, :, H:W] = total[k, W : 2 * W]
            diag_ref[k] = unpack(total.at[k, pl.ds(2 * W, PACK)])

    def body(p):
        @pl.when(composing & (first_sender(p) | (quads & second_sender(p))))
        def _():
            for copy in step_copies(p, 0):
                copy.wait_send()

        @pl.when(lower & head(p))
        def _():
            for copy in step_copies(p, 2):
                copy.wait_send()

        @pl.when((quads & head(p)) | ((m == 0) & (g == 3)))
        def _():
            for when, copy in head_copies(p, head_out):
                pl.when(when)(copy.wait_send)

        for when, copy in relay_copies(p):
            pl.when(when)(copy.wait_send)

        @pl.when(composing & ((plus(p) & (g == 1)) | (~plus(p) & (g == 0))))
        def _():
            pair_copy(p, 1).wait_send()

        @pl.when(passes_on & ((m > 0) | (g < 3)))
        def _():
            own_copy(p).wait_send()

    both(body)
    for k in range(2):
        for step in range(1, 8):
            send_part(k, step).wait_send()
        for copy in first_totals(k):
            copy.wait_send()
        for step in (2, 6, 4):
            pass_on(k, step).wait_send()


def local(nodes, pivot_inverse, factor_block, live_width_array, pole_weight):
    vmem = pl.BlockSpec(memory_space=pltpu.VMEM)
    hbm = pl.BlockSpec(memory_space=pltpu.HBM)
    dma = pltpu.SemaphoreType.DMA
    packed = pltpu.VMEM((2, 2, PACK, H), F32)
    return pl.pallas_call(
        functools.partial(kernel, nodes),
        out_shape=[jax.ShapeDtypeStruct((2, W, W), F32)] * 2,
        in_specs=[hbm, hbm, hbm, hbm],
        out_specs=[vmem, vmem],
        scratch_shapes=[
            pltpu.VMEM((2, 2, 2, W, W), F32),
            pltpu.VMEM((2, 2, 2, W, W), F32),
            pltpu.SMEM((2,), jnp.int32),
            pltpu.SMEM((2, 2), F32),
            pltpu.VMEM((2, 2, 4, W, W), BF),
            pltpu.VMEM((2, 7, 4, W, W), BF),
            pltpu.VMEM((2, 7, 2, W, W), F32),
            pltpu.VMEM((2, 3, 2, W, W), F32),
            pltpu.VMEM((2, 3, 2, PACK, H), F32),
            pltpu.VMEM((2, 2, 2, W, W), F32),
            pltpu.VMEM((2, 2, 2, PACK, H), F32),
            packed,
            packed,
            packed,
            packed,
            packed,
            pltpu.VMEM((2, 2, W, W), F32),
            pltpu.VMEM((2, ROWS, H), F32),
            pltpu.VMEM((2, 7, PART, H), F32),
            pltpu.VMEM((2, ROWS, H), F32),
            pltpu.VMEM((PACK, H), F32),
            dma((6,)),
            dma((2, 10)),
            dma((2, 8)),
            dma((2, 7)),
            dma((2, 7)),
            dma((2, 7)),
            dma((2, 7)),
        ],
        compiler_params=pltpu.CompilerParams(
            collective_id=0, has_side_effects=True, vmem_limit_bytes=VMEM_MIB << 20
        ),
        name="selected_inversion",
    )(live_width_array, pole_weight, pivot_inverse, factor_block)


def solution(mesh):
    placed = (
        P("pole", "snode", None, None, None),
        P("pole", "snode", None, None, None),
        P("snode"),
        P("pole", None),
    )
    return jax.shard_map(
        functools.partial(local, mesh.shape["snode"]),
        mesh=mesh,
        in_specs=placed,
        out_specs=(P("snode", None, None), P("snode", None, None)),
        check_vma=False,
    )
```

```python
import functools

import jax
import jax.numpy as jnp
from jax import lax
from jax.experimental import pallas as pl
from jax.experimental.pallas import tpu as pltpu
from jax.sharding import PartitionSpec as P

MESH = pl.DeviceIdType.MESH
F32 = jnp.float32
BF = jnp.bfloat16
W = 256
H = 128
PACK = 264
PART = 104
ROWS = 8 * PART
GROUP = 4
VMEM_MIB = 52
OWN, GOT1, PAIR, GOT2, QUAD, GOT3, OCT, AHEAD, AHEAD8 = range(9)
NEAR = (1, 2, 4, 5, 7, 8)


def split(x):
    high = x.astype(BF)
    return high, (x - high.astype(F32)).astype(BF)


def csplit(pair):
    return split(pair[0]) + split(pair[1])


def dot(a, b):
    return jnp.dot(a, b, preferred_element_type=F32)


def dot_t(a, b):
    return lax.dot_general(a, b, (((0,), (0,)), ((), ())), preferred_element_type=F32)


def product(left, right, mul=dot):
    lrh, lrl, lih, lil = left
    rrh, rrl, rih, ril = right
    real = mul(lrh, rrh) - mul(lih, rih)
    real += (mul(lrl, rrh) + mul(lrh, rrl)) - (mul(lil, rih) + mul(lih, ril))
    imag = mul(lrh, rih) + mul(lih, rrh)
    imag += (mul(lrl, rih) + mul(lrh, ril)) + (mul(lil, rrh) + mul(lih, rrl))
    return real, imag


def sandwich(middle, outer):
    return product(outer, csplit(product(csplit(middle), outer)), dot_t)


def tri():
    row = lax.broadcasted_iota(jnp.int32, (H, H), 0)
    col = lax.broadcasted_iota(jnp.int32, (H, H), 1)
    return row, col


def pack_into(ref, block):
    row, col = tri()
    last = block[H:, H:]
    ref[0:H, :] = block[:H, H:]
    ref[H : 2 * H, :] = jnp.where(row <= col, block[:H, :H], last)
    diagonal = jnp.sum(jnp.where(row == col, last, 0.0), axis=0, keepdims=True)
    ref[2 * H : PACK, :] = jnp.broadcast_to(diagonal, (8, H))


def unpack(ref):
    row, col = tri()
    upper = ref[0:H, :]
    both = ref[H : 2 * H, :]
    both_t = both.T
    diagonal = ref[2 * H : 2 * H + 1, :]
    first = jnp.where(row <= col, both, both_t)
    last = jnp.where(row > col, both, jnp.where(row == col, diagonal, both_t))
    return jnp.concatenate(
        [jnp.concatenate([first, upper], 1), jnp.concatenate([upper.T, last], 1)], 0
    )


def unpack2(ref):
    return unpack(ref.at[0]), unpack(ref.at[1])


def pack2(ref, pair):
    pack_into(ref.at[0], pair[0])
    pack_into(ref.at[1], pair[1])


def kernel(
    nodes,
    width_hbm,
    weight_hbm,
    p_hbm,
    f_hbm,
    diag_ref,
    off_ref,
    p_ref,
    f_ref,
    width_ref,
    weight_ref,
    fs,
    steps_a,
    steps_b,
    got_a,
    got_b,
    out_a,
    out_b,
    jump,
    entry,
    head_out,
    pair_out,
    own_out,
    s_in,
    dens,
    parts,
    total,
    spare,
    load_sem,
    sent,
    got,
    rs_send,
    rs_recv,
    ag_send,
    ag_recv,
):
    me = lax.axis_index("pole")
    core = lax.rem(me, 2)
    i = lax.axis_index("snode")
    groups = nodes // GROUP
    g = lax.rem(i, GROUP)
    m = lax.div(i, GROUP)
    low = 1 - lax.rem(m, 2)

    loads = [
        pltpu.make_async_copy(width_hbm, width_ref, load_sem.at[0]),
        pltpu.make_async_copy(weight_hbm, weight_ref, load_sem.at[1]),
    ]
    for p in range(2):
        loads.append(pltpu.make_async_copy(f_hbm.at[p], f_ref.at[p], load_sem.at[2 + 2 * p]))
        loads.append(pltpu.make_async_copy(p_hbm.at[p], p_ref.at[p], load_sem.at[3 + 2 * p]))
    for load in loads:
        load.start()

    barrier = pltpu.get_barrier_semaphore()
    for step in NEAR:
        for near in (lax.rem(i + step, nodes), lax.rem(i + nodes - step, nodes)):
            pl.semaphore_signal(barrier, inc=1, device_id=(me, near), device_id_type=MESH)
    for step in range(1, 8):
        pl.semaphore_signal(
            barrier, inc=1, device_id=(lax.rem(me + step, 8), i), device_id_type=MESH
        )

    row = lax.broadcasted_iota(jnp.int32, (W, W), 0)
    col = lax.broadcasted_iota(jnp.int32, (W, W), 1)

    def pivot(p, k):
        live = (row < width_ref[k]) & (col < width_ref[k])
        return tuple(jnp.where(live, p_ref[p, k, part], 0.0) for part in range(2))

    def load4(ref):
        return tuple(ref[n] for n in range(4))

    def store4(ref, four):
        for n in range(4):
            ref[n] = four[n]

    def both(body):
        def turn(n, carry):
            body(n)
            return carry

        lax.fori_loop(0, 2, turn, 0)

    def plus(p, low=low):
        return lax.rem(p + low, 2) == 1

    def first_sender(p):
        return lax.rem(g + lax.rem(p + low, 2), 2) == 1

    def second_sender(p):
        return (plus(p) & (g == 1)) | (~plus(p) & (g == 2))

    def head(p):
        return (plus(p) & (g == 3)) | (~plus(p) & (g == 0))

    composing = m > 0
    quads = composing & (m < groups - 1)
    final = m == groups - 1
    lower = m == 4
    upper = m == 5

    def second(p):
        return quads | (final & plus(p))

    def direct(p):
        return composing & plus(p) & ((g == 3) | (g == 1))

    def passes(p):
        return (m == 0) | (((g == 0) | (g == 2)) & ~plus(p))

    def remote(src, dst, p, kind, landing, to):
        return pltpu.make_async_remote_copy(
            src_ref=src,
            dst_ref=dst,
            send_sem=sent.at[p, kind],
            recv_sem=got.at[p, landing],
            device_id=(me, to),
            device_id_type=MESH,
        )

    def step_copies(p, level):
        out = jnp.int32(0) if level < 2 else jnp.int32(1)
        way = jnp.where(plus(p), 1, -1)
        if level == 2:
            to = jnp.where(plus(p), i + 1, i + 7)
        else:
            to = i + way * (level + 1)
        to = lax.rem(to + nodes, nodes)
        return [
            remote(out_a.at[p, out], got_a.at[p, level], p, 2 * (level // 2), 2 * level, to),
            remote(out_b.at[p, out], got_b.at[p, level], p, 2 * (level // 2) + 1, 2 * level + 1, to),
        ]

    def post_a(p, level, a_pair):
        out = 0 if level < 2 else 1
        out_a[p, out, 0] = a_pair[0]
        out_a[p, out, 1] = a_pair[1]

    def post_b(p, level, slot):
        out = 0 if level < 2 else 1
        pack2(out_b.at[p, out], (steps_b[p, slot, 0], steps_b[p, slot, 1]))

    def head_copies(p, src):
        n = m + 1
        forward = lax.rem(p + 1 - lax.rem(n, 2), 2) == 1
        base = GROUP * n
        ahead = jnp.where(
            n == 4, base + 4 + 3 * p, base + jnp.where((n == 5) | (n == groups - 1), 1, 3)
        )
        to_jump = (n < groups) & (forward | (n == 4))
        final_next = n == groups - 1
        to_entry = (n < groups) & ~to_jump
        return [
            (to_jump, remote(src.at[p], jump.at[p], p, 4, 6, lax.rem(ahead, nodes))),
            (to_entry, remote(src.at[p], entry.at[p], p, 4, 7, lax.rem(base, nodes))),
            ((n == 4) & forward, remote(src.at[p], jump.at[p], p, 6, 6, lax.rem(base + 3, nodes))),
            (final_next & forward, remote(src.at[p], jump.at[p], p, 6, 6, lax.rem(base + 3, nodes))),
            ((n == 4) & ~forward, remote(src.at[p], entry.at[p], p, 6, 7, lax.rem(base, nodes))),
        ]

    def send_head(p, src):
        for when, copy in head_copies(p, src):
            pl.when(when)(copy.start)

    def relay_copies(p):
        to_jump = quads & ~upper & plus(p) & (g == 3)
        to_entry = composing & plus(p) & (g == 1)
        return [
            (to_jump, remote(jump.at[p], jump.at[p], p, 5, 6, lax.rem(i + nodes - 2, nodes))),
            (to_entry, remote(jump.at[p], entry.at[p], p, 5, 7, lax.rem(i + nodes - 1, nodes))),
        ]

    def pair_copy(p, ahead):
        return remote(pair_out.at[p], entry.at[p], p, 8, 7, lax.rem(i + ahead, nodes))

    def own_copy(p):
        return remote(own_out.at[p], entry.at[p], p, 9, 7, lax.rem(i + 1, nodes))

    with jax.named_scope("own_steps"):
        loads[0].wait()
        for p in range(2):
            loads[2 + 2 * p].wait()
            for k in range(2):
                live = col < width_ref[k]
                store4(
                    fs.at[p, k],
                    csplit([jnp.where(live, f_ref[p, k, part], 0.0) for part in range(2)]),
                )
            real, imag = product(load4(fs.at[p, 0]), load4(fs.at[p, 1]))
            store4(steps_a.at[p, OWN], csplit((real, imag)))

            if p == 0:

                @pl.when(low == 0)
                def _():
                    pl.semaphore_wait(barrier, 2 * len(NEAR) + 7)

            @pl.when(composing & first_sender(p))
            def _():
                post_a(p, 0, (real, imag))

                @pl.when(low == 0)
                def _():
                    step_copies(p, 0)[0].start()

        for p in range(2):
            loads[3 + 2 * p].wait()
            inner = sandwich(pivot(p, 0), load4(fs.at[p, 1]))
            last = pivot(p, 1)
            for part in range(2):
                steps_b[p, OWN, part] = last[part] + inner[part]

            @pl.when(composing & first_sender(p))
            def _():
                post_b(p, 0, OWN)

                @pl.when(low == 0)
                def _():
                    step_copies(p, 0)[1].start()

        @pl.when(low == 1)
        def _():
            pl.semaphore_wait(barrier, 2 * len(NEAR) + 7)
            for p in range(2):

                @pl.when(composing & first_sender(p))
                def _():
                    for copy in step_copies(p, 0):
                        copy.start()


    def merge(p, level, own, received, new, forward, sends):
        copies = step_copies(p, level)
        copies[0].wait_recv()
        store4(steps_a.at[p, received], csplit((got_a[p, level, 0], got_a[p, level, 1])))
        first = jnp.where(forward, received, own)
        second = jnp.where(forward, own, received)
        a_pair = product(load4(steps_a.at[p, first]), load4(steps_a.at[p, second]))
        store4(steps_a.at[p, new], csplit(a_pair))
        if sends is not None:

            @pl.when(sends)
            def _():
                post_a(p, level + 1, a_pair)
                step_copies(p, level + 1)[0].start()

        copies[1].wait_recv()
        block = unpack2(got_b.at[p, level])
        steps_b[p, received, 0] = block[0]
        steps_b[p, received, 1] = block[1]
        inner = sandwich((steps_b[p, first, 0], steps_b[p, first, 1]), load4(steps_a.at[p, second]))
        for part in range(2):
            steps_b[p, new, part] = steps_b[p, second, part] + inner[part]
        if sends is not None:

            @pl.when(sends)
            def _():
                post_b(p, level + 1, new)
                step_copies(p, level + 1)[1].start()

    with jax.named_scope("pairs"):

        @pl.when(composing)
        def _():
            def body(p):
                @pl.when(~first_sender(p))
                def _():
                    merge(p, 0, OWN, GOT1, PAIR, plus(p), second(p) & second_sender(p))

            both(body)

    with jax.named_scope("quads"):

        @pl.when(composing)
        def _():
            def body(p):
                @pl.when(second(p) & head(p))
                def _():
                    merge(p, 1, PAIR, GOT2, QUAD, plus(p), lower)

            both(body)

    with jax.named_scope("octs"):

        @pl.when(upper)
        def _():
            def body(p):
                @pl.when(head(p))
                def _():
                    merge(p, 2, QUAD, GOT3, OCT, True, None)

            both(body)

    def advanced(p, slot, state):
        inner = sandwich(state, load4(steps_a.at[p, slot]))
        return steps_b[p, slot, 0] + inner[0], steps_b[p, slot, 1] + inner[1]

    def advance(p, slot, state, ref):
        pack2(ref, advanced(p, slot, state))

    def compose(p, first, second, new):
        outer = load4(steps_a.at[p, second])
        store4(steps_a.at[p, new], csplit(product(load4(steps_a.at[p, first]), outer)))
        inner = sandwich((steps_b[p, first, 0], steps_b[p, first, 1]), outer)
        for part in range(2):
            steps_b[p, new, part] = steps_b[p, second, part] + inner[part]

    def jumps(p):
        forward = plus(p) & ((g == 1) | ((g == 3) & quads))
        return composing & (forward | (upper & head(p)))

    with jax.named_scope("jumps"):

        def body(p):
            @pl.when(jumps(p))
            def _():
                remote(jump.at[p], jump.at[p], p, 4, 6, i).wait_recv()
                for when, copy in relay_copies(p):
                    pl.when(when)(copy.start)
                state = unpack2(jump.at[p])

                @pl.when(g == 1)
                def _():
                    advance(p, PAIR, state, pair_out.at[p])
                    pair_copy(p, 1).start()

                @pl.when(g != 1)
                def _():
                    advance(p, jnp.where(upper, OCT, QUAD), state, head_out.at[p])
                    send_head(p, head_out)

        both(body)

    with jax.named_scope("steps_ahead"):

        def body(p):
            @pl.when(direct(p) & (g == 3))
            def _():
                compose(p, GOT2, GOT1, AHEAD)

                @pl.when(upper)
                def _():
                    compose(p, GOT3, AHEAD, AHEAD8)

        both(body)

    def send_part(k, step):
        to = lax.rem(me + step, 8)
        return pltpu.make_async_remote_copy(
            src_ref=dens.at[k, pl.ds(pl.multiple_of(to * PART, 8), PART)],
            dst_ref=parts.at[k, step - 1],
            send_sem=rs_send.at[k, step - 1],
            recv_sem=rs_recv.at[k, step - 1],
            device_id=(to, i),
            device_id_type=MESH,
        )

    sibling = me + 1 - 2 * core

    def send_total(k, owner, to, slot):
        rows = pl.ds(pl.multiple_of(owner * PART, 8), PART)
        return pltpu.make_async_remote_copy(
            src_ref=total.at[k, rows],
            dst_ref=total.at[k, rows],
            send_sem=ag_send.at[k, slot],
            recv_sem=ag_recv.at[k, slot],
            device_id=(to, i),
            device_id_type=MESH,
        )

    def same_core(step):
        return lax.rem(me + step, 8)

    def first_totals(k):
        copies = [send_total(k, me, same_core(step), step - 1) for step in (4, 2, 6)]
        return copies + [send_total(k, me, sibling, 0)]

    order = (4, 3, 5, 2, 6, 7, 1)

    def put(n, p, k, product_pair, inverse_pair):
        re_w, im_w = weight_ref[p, 0], weight_ref[p, 1]
        off = -(re_w * product_pair[1] + im_w * product_pair[0])
        diag = re_w * inverse_pair[1] + im_w * inverse_pair[0]
        mine = dens.at[k]
        if n == 0:
            mine[0:W, :] = off[:, :H]
            mine[W : 2 * W, :] = off[:, H:]
            pack_into(mine.at[pl.ds(2 * W, PACK)], diag)
            mine[2 * W + PACK : ROWS, :] = jnp.zeros((ROWS - 2 * W - PACK, H), F32)
        else:
            mine[0:W, :] += off[:, :H]
            mine[W : 2 * W, :] += off[:, H:]
            pack_into(spare, diag)
            mine[2 * W : 2 * W + PACK, :] += spare[...]
            for step in order:
                send_part(k, step).start()

    loads[1].wait()

    later = composing & (g == 0)

    def enter(p, hold):
        @pl.when(i == 0)
        def _():
            s_in[p] = jnp.zeros_like(s_in[p])
            pack2(own_out.at[p], (steps_b[p, OWN, 0], steps_b[p, OWN, 1]))
            own_copy(p).start()

        @pl.when((i > 0) & ~direct(p))
        def _():
            remote(entry.at[p], entry.at[p], p, 7, 7, i).wait_recv()
            block = unpack2(entry.at[p])
            s_in[p, 0] = block[0]
            s_in[p, 1] = block[1]

        @pl.when(direct(p))
        def _():
            @pl.when(final & (g == 3))
            def _():
                remote(jump.at[p], jump.at[p], p, 4, 6, i).wait_recv()

            slot = jnp.where(g == 1, GOT1, jnp.where(upper, AHEAD8, AHEAD))
            block = advanced(p, slot, unpack2(jump.at[p]))
            s_in[p, 0] = block[0]
            s_in[p, 1] = block[1]

        @pl.when(composing & (g == 0) & ~plus(p))
        def _():
            @pl.when(quads & ~upper)
            def _():
                advance(p, QUAD, (s_in[p, 0], s_in[p, 1]), head_out.at[p])
                send_head(p, head_out)

            advance(p, PAIR, (s_in[p, 0], s_in[p, 1]), pair_out.at[p])
            pair_copy(p, 2).start()

        @pl.when(passes(p) & (i > 0))
        def _():
            advance(p, OWN, (s_in[p, 0], s_in[p, 1]), own_out.at[p])

            @pl.when(((m > 0) | (g < 3)) & ~(later & hold))
            def _():
                own_copy(p).start()

            @pl.when((m == 0) & (g == 3))
            def _():
                send_head(p, own_out)

    def details(n, p):
        state = (s_in[p, 0], s_in[p, 1])
        for k in range(2):
            link = load4(fs.at[p, k])
            moved = product(csplit(state), link)
            inner = product(link, csplit(moved), dot_t)
            block = pivot(p, k)
            state = (block[0] + inner[0], block[1] + inner[1])
            put(n, p, k, moved, state)

    with jax.named_scope("states"):
        flip = jnp.where(composing, lax.rem(g, 2), 0)
        one, two = lax.rem(low + flip, 2), lax.rem(low + flip + 1, 2)
        enter(one, True)

        @pl.when(composing)
        def _():
            details(0, one)

            @pl.when(later & (core == 0))
            def _():
                own_copy(one).start()

        enter(two, False)

        @pl.when(m == 0)
        def _():
            details(0, one)

    with jax.named_scope("last_details"):
        details(1, two)

        @pl.when(later & (core == 1))
        def _():
            own_copy(one).start()

    with jax.named_scope("pole_sum"):
        mine = pl.ds(pl.multiple_of(me * PART, 8), PART)
        for k in range(2):
            acc = dens[k, mine]
            for step in range(1, 8):
                send_part(k, step).wait_recv()
                acc = acc + parts[k, step - 1]
            total[k, mine] = acc
            for copy in first_totals(k):
                copy.start()
    with jax.named_scope("pole_gather"):
        def pass_on(k, step):
            return send_total(k, lax.rem(me + 8 - step, 8), sibling, step)

        for k in range(2):
            for step in (2, 6, 4):
                send_total(k, lax.rem(me + 8 - step, 8), me, step - 1).wait_recv()
                pass_on(k, step).start()
        for k in range(2):
            send_total(k, sibling, me, 0).wait_recv()
            for step in (2, 6, 4):
                send_total(k, lax.rem(sibling + 8 - step, 8), me, step).wait_recv()
            off_ref[k, :, 0:H] = total[k, 0:W]
            off_ref[k, :, H:W] = total[k, W : 2 * W]
            diag_ref[k] = unpack(total.at[k, pl.ds(2 * W, PACK)])

    def body(p):
        @pl.when(composing & (first_sender(p) | (second(p) & second_sender(p))))
        def _():
            for copy in step_copies(p, 0):
                copy.wait_send()

        @pl.when(lower & head(p))
        def _():
            for copy in step_copies(p, 2):
                copy.wait_send()

        @pl.when((quads & head(p)) | ((m == 0) & (g == 3)))
        def _():
            for when, copy in head_copies(p, head_out):
                pl.when(when)(copy.wait_send)

        for when, copy in relay_copies(p):
            pl.when(when)(copy.wait_send)

        @pl.when(composing & ((plus(p) & (g == 1)) | (~plus(p) & (g == 0))))
        def _():
            pair_copy(p, 1).wait_send()

        @pl.when(passes(p) & ((m > 0) | (g < 3)))
        def _():
            own_copy(p).wait_send()

    both(body)
    for k in range(2):
        for step in range(1, 8):
            send_part(k, step).wait_send()
        for copy in first_totals(k):
            copy.wait_send()
        for step in (2, 6, 4):
            pass_on(k, step).wait_send()


def local(nodes, pivot_inverse, factor_block, live_width_array, pole_weight):
    vmem = pl.BlockSpec(memory_space=pltpu.VMEM)
    hbm = pl.BlockSpec(memory_space=pltpu.HBM)
    dma = pltpu.SemaphoreType.DMA
    packed = pltpu.VMEM((2, 2, PACK, H), F32)
    return pl.pallas_call(
        functools.partial(kernel, nodes),
        out_shape=[jax.ShapeDtypeStruct((2, W, W), F32)] * 2,
        in_specs=[hbm, hbm, hbm, hbm],
        out_specs=[vmem, vmem],
        scratch_shapes=[
            pltpu.VMEM((2, 2, 2, W, W), F32),
            pltpu.VMEM((2, 2, 2, W, W), F32),
            pltpu.SMEM((2,), jnp.int32),
            pltpu.SMEM((2, 2), F32),
            pltpu.VMEM((2, 2, 4, W, W), BF),
            pltpu.VMEM((2, 9, 4, W, W), BF),
            pltpu.VMEM((2, 9, 2, W, W), F32),
            pltpu.VMEM((2, 3, 2, W, W), F32),
            pltpu.VMEM((2, 3, 2, PACK, H), F32),
            pltpu.VMEM((2, 2, 2, W, W), F32),
            pltpu.VMEM((2, 2, 2, PACK, H), F32),
            packed,
            packed,
            packed,
            packed,
            packed,
            pltpu.VMEM((2, 2, W, W), F32),
            pltpu.VMEM((2, ROWS, H), F32),
            pltpu.VMEM((2, 7, PART, H), F32),
            pltpu.VMEM((2, ROWS, H), F32),
            pltpu.VMEM((PACK, H), F32),
            dma((6,)),
            dma((2, 10)),
            dma((2, 8)),
            dma((2, 7)),
            dma((2, 7)),
            dma((2, 7)),
            dma((2, 7)),
        ],
        compiler_params=pltpu.CompilerParams(
            collective_id=0, has_side_effects=True, vmem_limit_bytes=VMEM_MIB << 20
        ),
        name="selected_inversion",
    )(live_width_array, pole_weight, pivot_inverse, factor_block)


def solution(mesh):
    placed = (
        P("pole", "snode", None, None, None),
        P("pole", "snode", None, None, None),
        P("snode"),
        P("pole", None),
    )
    return jax.shard_map(
        functools.partial(local, mesh.shape["snode"]),
        mesh=mesh,
        in_specs=placed,
        out_specs=(P("snode", None, None), P("snode", None, None)),
        check_vma=False,
    )
```

```python
import functools

import jax
import jax.numpy as jnp
from jax import lax
from jax.experimental import pallas as pl
from jax.experimental.pallas import tpu as pltpu
from jax.sharding import PartitionSpec as P

MESH = pl.DeviceIdType.MESH
F32 = jnp.float32
BF = jnp.bfloat16
W = 256
H = 128
PACK = 264
PART = 104
ROWS = 8 * PART
GROUP = 4
VMEM_MIB = 52
OWN, GOT1, PAIR, GOT2, QUAD, GOT3, OCT, AHEAD, AHEAD8 = range(9)
NEAR = (1, 2, 4, 5, 7, 8)


def split(x):
    high = x.astype(BF)
    return high, (x - high.astype(F32)).astype(BF)


def csplit(pair):
    return split(pair[0]) + split(pair[1])


def dot(a, b):
    return jnp.dot(a, b, preferred_element_type=F32)


def dot_t(a, b):
    return lax.dot_general(a, b, (((0,), (0,)), ((), ())), preferred_element_type=F32)


def product(left, right, mul=dot):
    lrh, lrl, lih, lil = left
    rrh, rrl, rih, ril = right
    real = mul(lrh, rrh) - mul(lih, rih)
    real += (mul(lrl, rrh) + mul(lrh, rrl)) - (mul(lil, rih) + mul(lih, ril))
    imag = mul(lrh, rih) + mul(lih, rrh)
    imag += (mul(lrl, rih) + mul(lrh, ril)) + (mul(lil, rrh) + mul(lih, rrl))
    return real, imag


def sandwich(middle, outer):
    return product(outer, csplit(product(csplit(middle), outer)), dot_t)


def tri():
    row = lax.broadcasted_iota(jnp.int32, (H, H), 0)
    col = lax.broadcasted_iota(jnp.int32, (H, H), 1)
    return row, col


def pack_into(ref, block):
    row, col = tri()
    last = block[H:, H:]
    ref[0:H, :] = block[:H, H:]
    ref[H : 2 * H, :] = jnp.where(row <= col, block[:H, :H], last)
    diagonal = jnp.sum(jnp.where(row == col, last, 0.0), axis=0, keepdims=True)
    ref[2 * H : PACK, :] = jnp.broadcast_to(diagonal, (8, H))


def unpack(ref):
    row, col = tri()
    upper = ref[0:H, :]
    both = ref[H : 2 * H, :]
    both_t = both.T
    diagonal = ref[2 * H : 2 * H + 1, :]
    first = jnp.where(row <= col, both, both_t)
    last = jnp.where(row > col, both, jnp.where(row == col, diagonal, both_t))
    return jnp.concatenate(
        [jnp.concatenate([first, upper], 1), jnp.concatenate([upper.T, last], 1)], 0
    )


def unpack2(ref):
    return unpack(ref.at[0]), unpack(ref.at[1])


def pack2(ref, pair):
    pack_into(ref.at[0], pair[0])
    pack_into(ref.at[1], pair[1])


def kernel(
    nodes,
    width_hbm,
    weight_hbm,
    p_hbm,
    f_hbm,
    diag_ref,
    off_ref,
    p_ref,
    f_ref,
    width_ref,
    weight_ref,
    fs,
    steps_a,
    steps_b,
    got_a,
    got_b,
    out_a,
    out_b,
    jump,
    entry,
    head_out,
    pair_out,
    own_out,
    s_in,
    dens,
    parts,
    total,
    spare,
    load_sem,
    sent,
    got,
    rs_send,
    rs_recv,
    ag_send,
    ag_recv,
):
    me = lax.axis_index("pole")
    core = lax.rem(me, 2)
    i = lax.axis_index("snode")
    groups = nodes // GROUP
    g = lax.rem(i, GROUP)
    m = lax.div(i, GROUP)
    low = 1 - lax.rem(m, 2)

    loads = [
        pltpu.make_async_copy(width_hbm, width_ref, load_sem.at[0]),
        pltpu.make_async_copy(weight_hbm, weight_ref, load_sem.at[1]),
    ]
    for p in range(2):
        loads.append(pltpu.make_async_copy(f_hbm.at[p], f_ref.at[p], load_sem.at[2 + 2 * p]))
        loads.append(pltpu.make_async_copy(p_hbm.at[p], p_ref.at[p], load_sem.at[3 + 2 * p]))
    for load in loads:
        load.start()

    barrier = pltpu.get_barrier_semaphore()
    for step in NEAR:
        for near in (lax.rem(i + step, nodes), lax.rem(i + nodes - step, nodes)):
            pl.semaphore_signal(barrier, inc=1, device_id=(me, near), device_id_type=MESH)
    for step in range(1, 8):
        pl.semaphore_signal(
            barrier, inc=1, device_id=(lax.rem(me + step, 8), i), device_id_type=MESH
        )

    row = lax.broadcasted_iota(jnp.int32, (W, W), 0)
    col = lax.broadcasted_iota(jnp.int32, (W, W), 1)

    def pivot(p, k):
        live = (row < width_ref[k]) & (col < width_ref[k])
        return tuple(jnp.where(live, p_ref[p, k, part], 0.0) for part in range(2))

    def load4(ref):
        return tuple(ref[n] for n in range(4))

    def store4(ref, four):
        for n in range(4):
            ref[n] = four[n]

    def both(body):
        def turn(n, carry):
            body(n)
            return carry

        lax.fori_loop(0, 2, turn, 0)

    def plus(p, low=low):
        return lax.rem(p + low, 2) == 1

    def first_sender(p):
        return lax.rem(g + lax.rem(p + low, 2), 2) == 1

    def second_sender(p):
        return (plus(p) & (g == 1)) | (~plus(p) & (g == 2))

    def head(p):
        return (plus(p) & (g == 3)) | (~plus(p) & (g == 0))

    composing = m > 0
    quads = composing & (m < groups - 1)
    final = m == groups - 1
    lower = m == 4
    upper = m == 5

    def second(p):
        return quads | (final & plus(p))

    def direct(p):
        return composing & plus(p) & ((g == 3) | (g == 1))

    def passes(p):
        return (m == 0) | (((g == 0) | (g == 2)) & ~plus(p))

    def remote(src, dst, p, kind, landing, to):
        return pltpu.make_async_remote_copy(
            src_ref=src,
            dst_ref=dst,
            send_sem=sent.at[p, kind],
            recv_sem=got.at[p, landing],
            device_id=(me, to),
            device_id_type=MESH,
        )

    def step_copies(p, level):
        out = jnp.int32(0) if level < 2 else jnp.int32(1)
        way = jnp.where(plus(p), 1, -1)
        if level == 2:
            to = jnp.where(plus(p), i + 1, i + 7)
        else:
            to = i + way * (level + 1)
        to = lax.rem(to + nodes, nodes)
        return [
            remote(out_a.at[p, out], got_a.at[p, level], p, 2 * (level // 2), 2 * level, to),
            remote(out_b.at[p, out], got_b.at[p, level], p, 2 * (level // 2) + 1, 2 * level + 1, to),
        ]

    def post_a(p, level, a_pair):
        out = 0 if level < 2 else 1
        out_a[p, out, 0] = a_pair[0]
        out_a[p, out, 1] = a_pair[1]

    def post_b(p, level, slot):
        out = 0 if level < 2 else 1
        pack2(out_b.at[p, out], (steps_b[p, slot, 0], steps_b[p, slot, 1]))

    def head_copies(p, src):
        n = m + 1
        forward = lax.rem(p + 1 - lax.rem(n, 2), 2) == 1
        base = GROUP * n
        ahead = jnp.where(
            n == 4, base + 4 + 3 * p, base + jnp.where((n == 5) | (n == groups - 1), 1, 3)
        )
        to_jump = (n < groups) & (forward | (n == 4))
        final_next = n == groups - 1
        to_entry = (n < groups) & ~to_jump
        return [
            (to_jump, remote(src.at[p], jump.at[p], p, 4, 6, lax.rem(ahead, nodes))),
            (to_entry, remote(src.at[p], entry.at[p], p, 4, 7, lax.rem(base, nodes))),
            ((n == 4) & forward, remote(src.at[p], jump.at[p], p, 6, 6, lax.rem(base + 3, nodes))),
            (final_next & forward, remote(src.at[p], jump.at[p], p, 6, 6, lax.rem(base + 3, nodes))),
            ((n == 4) & ~forward, remote(src.at[p], entry.at[p], p, 6, 7, lax.rem(base, nodes))),
        ]

    def send_head(p, src):
        for when, copy in head_copies(p, src):
            pl.when(when)(copy.start)

    def relay_copies(p):
        to_jump = quads & ~upper & plus(p) & (g == 3)
        to_entry = composing & plus(p) & (g == 1)
        return [
            (to_jump, remote(jump.at[p], jump.at[p], p, 5, 6, lax.rem(i + nodes - 2, nodes))),
            (to_entry, remote(jump.at[p], entry.at[p], p, 5, 7, lax.rem(i + nodes - 1, nodes))),
        ]

    def pair_copy(p, ahead):
        return remote(pair_out.at[p], entry.at[p], p, 8, 7, lax.rem(i + ahead, nodes))

    def own_copy(p):
        return remote(own_out.at[p], entry.at[p], p, 9, 7, lax.rem(i + 1, nodes))

    with jax.named_scope("own_steps"):
        loads[0].wait()
        for p in range(2):
            loads[2 + 2 * p].wait()
            for k in range(2):
                live = col < width_ref[k]
                store4(
                    fs.at[p, k],
                    csplit([jnp.where(live, f_ref[p, k, part], 0.0) for part in range(2)]),
                )
            real, imag = product(load4(fs.at[p, 0]), load4(fs.at[p, 1]))
            store4(steps_a.at[p, OWN], csplit((real, imag)))

            if p == 0:

                @pl.when(low == 0)
                def _():
                    pl.semaphore_wait(barrier, 2 * len(NEAR) + 7)

            @pl.when(composing & first_sender(p))
            def _():
                post_a(p, 0, (real, imag))

                @pl.when(low == 0)
                def _():
                    step_copies(p, 0)[0].start()

        for p in range(2):
            loads[3 + 2 * p].wait()
            inner = sandwich(pivot(p, 0), load4(fs.at[p, 1]))
            last = pivot(p, 1)
            for part in range(2):
                steps_b[p, OWN, part] = last[part] + inner[part]

            @pl.when(composing & first_sender(p))
            def _():
                post_b(p, 0, OWN)

                @pl.when(low == 0)
                def _():
                    step_copies(p, 0)[1].start()

        @pl.when(low == 1)
        def _():
            pl.semaphore_wait(barrier, 2 * len(NEAR) + 7)
            for p in range(2):

                @pl.when(composing & first_sender(p))
                def _():
                    for copy in step_copies(p, 0):
                        copy.start()


    def merge(p, level, own, received, new, forward, sends):
        copies = step_copies(p, level)
        copies[0].wait_recv()
        store4(steps_a.at[p, received], csplit((got_a[p, level, 0], got_a[p, level, 1])))
        first = jnp.where(forward, received, own)
        second = jnp.where(forward, own, received)
        a_pair = product(load4(steps_a.at[p, first]), load4(steps_a.at[p, second]))
        store4(steps_a.at[p, new], csplit(a_pair))
        if sends is not None:

            @pl.when(sends)
            def _():
                post_a(p, level + 1, a_pair)
                step_copies(p, level + 1)[0].start()

        copies[1].wait_recv()
        block = unpack2(got_b.at[p, level])
        steps_b[p, received, 0] = block[0]
        steps_b[p, received, 1] = block[1]
        inner = sandwich((steps_b[p, first, 0], steps_b[p, first, 1]), load4(steps_a.at[p, second]))
        for part in range(2):
            steps_b[p, new, part] = steps_b[p, second, part] + inner[part]
        if sends is not None:

            @pl.when(sends)
            def _():
                post_b(p, level + 1, new)
                step_copies(p, level + 1)[1].start()

    def take_a(p, level, received):
        step_copies(p, level)[0].wait_recv()
        store4(steps_a.at[p, received], csplit((got_a[p, level, 0], got_a[p, level, 1])))

    def take_b(p, level, received):
        step_copies(p, level)[1].wait_recv()
        block = unpack2(got_b.at[p, level])
        steps_b[p, received, 0] = block[0]
        steps_b[p, received, 1] = block[1]

    def inner_into(p, first, second, new):
        inner = sandwich((steps_b[p, first, 0], steps_b[p, first, 1]), load4(steps_a.at[p, second]))
        steps_b[p, new, 0] = inner[0]
        steps_b[p, new, 1] = inner[1]

    def add_into(p, extra, new):
        for part in range(2):
            steps_b[p, new, part] += steps_b[p, extra, part]

    def gather(p):
        ahead = plus(p)
        take_a(p, 0, GOT1)
        first, second = jnp.where(ahead, GOT1, OWN), jnp.where(ahead, OWN, GOT1)
        pair = product(load4(steps_a.at[p, first]), load4(steps_a.at[p, second]))
        store4(steps_a.at[p, PAIR], csplit(pair))

        @pl.when(~ahead)
        def _():
            inner_into(p, OWN, GOT1, PAIR)

        take_a(p, 1, GOT2)
        first, second = jnp.where(ahead, GOT2, PAIR), jnp.where(ahead, PAIR, GOT2)
        quad = product(load4(steps_a.at[p, first]), load4(steps_a.at[p, second]))
        store4(steps_a.at[p, QUAD], csplit(quad))

        @pl.when(lower)
        def _():
            post_a(p, 2, quad)
            step_copies(p, 2)[0].start()

        @pl.when(ahead)
        def _():
            take_b(p, 1, GOT2)
            inner_into(p, GOT2, PAIR, QUAD)
            take_b(p, 0, GOT1)
            inner_into(p, GOT1, OWN, PAIR)
            add_into(p, OWN, PAIR)
            add_into(p, PAIR, QUAD)

        @pl.when(~ahead)
        def _():
            take_b(p, 0, GOT1)
            add_into(p, GOT1, PAIR)
            inner_into(p, PAIR, GOT2, QUAD)
            take_b(p, 1, GOT2)
            add_into(p, GOT2, QUAD)

        @pl.when(lower)
        def _():
            post_b(p, 2, QUAD)
            step_copies(p, 2)[1].start()

    with jax.named_scope("pairs"):

        @pl.when(composing)
        def _():
            def body(p):
                @pl.when(~first_sender(p) & ~(second(p) & head(p)))
                def _():
                    merge(p, 0, OWN, GOT1, PAIR, plus(p), second(p) & second_sender(p))

            both(body)

    with jax.named_scope("quads"):

        @pl.when(composing)
        def _():
            def body(p):
                @pl.when(second(p) & head(p))
                def _():
                    gather(p)

            both(body)

    with jax.named_scope("octs"):

        @pl.when(upper)
        def _():
            def body(p):
                @pl.when(head(p))
                def _():
                    merge(p, 2, QUAD, GOT3, OCT, True, None)

            both(body)

    def advanced(p, slot, state):
        inner = sandwich(state, load4(steps_a.at[p, slot]))
        return steps_b[p, slot, 0] + inner[0], steps_b[p, slot, 1] + inner[1]

    def advance(p, slot, state, ref):
        pack2(ref, advanced(p, slot, state))

    def compose(p, first, second, new):
        outer = load4(steps_a.at[p, second])
        store4(steps_a.at[p, new], csplit(product(load4(steps_a.at[p, first]), outer)))
        inner = sandwich((steps_b[p, first, 0], steps_b[p, first, 1]), outer)
        for part in range(2):
            steps_b[p, new, part] = steps_b[p, second, part] + inner[part]

    def jumps(p):
        forward = plus(p) & ((g == 1) | ((g == 3) & quads))
        return composing & (forward | (upper & head(p)))

    with jax.named_scope("jumps"):

        def body(p):
            @pl.when(jumps(p))
            def _():
                remote(jump.at[p], jump.at[p], p, 4, 6, i).wait_recv()
                for when, copy in relay_copies(p):
                    pl.when(when)(copy.start)
                state = unpack2(jump.at[p])

                @pl.when(g == 1)
                def _():
                    advance(p, PAIR, state, pair_out.at[p])
                    pair_copy(p, 1).start()

                @pl.when(g != 1)
                def _():
                    advance(p, jnp.where(upper, OCT, QUAD), state, head_out.at[p])
                    send_head(p, head_out)

        both(body)

    with jax.named_scope("steps_ahead"):

        def body(p):
            @pl.when(direct(p) & (g == 3))
            def _():
                compose(p, GOT2, GOT1, AHEAD)

                @pl.when(upper)
                def _():
                    compose(p, GOT3, AHEAD, AHEAD8)

        both(body)

    def send_part(k, step):
        to = lax.rem(me + step, 8)
        return pltpu.make_async_remote_copy(
            src_ref=dens.at[k, pl.ds(pl.multiple_of(to * PART, 8), PART)],
            dst_ref=parts.at[k, step - 1],
            send_sem=rs_send.at[k, step - 1],
            recv_sem=rs_recv.at[k, step - 1],
            device_id=(to, i),
            device_id_type=MESH,
        )

    sibling = me + 1 - 2 * core

    def send_total(k, owner, to, slot):
        rows = pl.ds(pl.multiple_of(owner * PART, 8), PART)
        return pltpu.make_async_remote_copy(
            src_ref=total.at[k, rows],
            dst_ref=total.at[k, rows],
            send_sem=ag_send.at[k, slot],
            recv_sem=ag_recv.at[k, slot],
            device_id=(to, i),
            device_id_type=MESH,
        )

    def same_core(step):
        return lax.rem(me + step, 8)

    def first_totals(k):
        copies = [send_total(k, me, same_core(step), step - 1) for step in (4, 2, 6)]
        return copies + [send_total(k, me, sibling, 0)]

    order = (4, 3, 5, 2, 6, 7, 1)

    def put(n, p, k, product_pair, inverse_pair):
        re_w, im_w = weight_ref[p, 0], weight_ref[p, 1]
        off = -(re_w * product_pair[1] + im_w * product_pair[0])
        diag = re_w * inverse_pair[1] + im_w * inverse_pair[0]
        mine = dens.at[k]
        if n == 0:
            mine[0:W, :] = off[:, :H]
            mine[W : 2 * W, :] = off[:, H:]
            pack_into(mine.at[pl.ds(2 * W, PACK)], diag)
            mine[2 * W + PACK : ROWS, :] = jnp.zeros((ROWS - 2 * W - PACK, H), F32)
        else:
            mine[0:W, :] += off[:, :H]
            mine[W : 2 * W, :] += off[:, H:]
            pack_into(spare, diag)
            mine[2 * W : 2 * W + PACK, :] += spare[...]
            for step in order:
                send_part(k, step).start()

    loads[1].wait()

    later = composing & (g == 0)

    def enter(p, hold):
        @pl.when(i == 0)
        def _():
            s_in[p] = jnp.zeros_like(s_in[p])
            pack2(own_out.at[p], (steps_b[p, OWN, 0], steps_b[p, OWN, 1]))
            own_copy(p).start()

        @pl.when((i > 0) & ~direct(p))
        def _():
            remote(entry.at[p], entry.at[p], p, 7, 7, i).wait_recv()
            block = unpack2(entry.at[p])
            s_in[p, 0] = block[0]
            s_in[p, 1] = block[1]

        @pl.when(direct(p))
        def _():
            @pl.when(final & (g == 3))
            def _():
                remote(jump.at[p], jump.at[p], p, 4, 6, i).wait_recv()

            slot = jnp.where(g == 1, GOT1, jnp.where(upper, AHEAD8, AHEAD))
            block = advanced(p, slot, unpack2(jump.at[p]))
            s_in[p, 0] = block[0]
            s_in[p, 1] = block[1]

        @pl.when(composing & (g == 0) & ~plus(p))
        def _():
            @pl.when(quads & ~upper)
            def _():
                advance(p, QUAD, (s_in[p, 0], s_in[p, 1]), head_out.at[p])
                send_head(p, head_out)

            advance(p, PAIR, (s_in[p, 0], s_in[p, 1]), pair_out.at[p])
            pair_copy(p, 2).start()

        @pl.when(passes(p) & (i > 0))
        def _():
            advance(p, OWN, (s_in[p, 0], s_in[p, 1]), own_out.at[p])

            @pl.when(((m > 0) | (g < 3)) & ~(later & hold))
            def _():
                own_copy(p).start()

            @pl.when((m == 0) & (g == 3))
            def _():
                send_head(p, own_out)

    def details(n, p):
        state = (s_in[p, 0], s_in[p, 1])
        for k in range(2):
            link = load4(fs.at[p, k])
            moved = product(csplit(state), link)
            inner = product(link, csplit(moved), dot_t)
            block = pivot(p, k)
            state = (block[0] + inner[0], block[1] + inner[1])
            put(n, p, k, moved, state)

    with jax.named_scope("states"):
        flip = jnp.where(composing, lax.rem(g, 2), 0)
        one, two = lax.rem(low + flip, 2), lax.rem(low + flip + 1, 2)
        enter(one, True)

        @pl.when(composing)
        def _():
            details(0, one)

            @pl.when(later & (core == 0))
            def _():
                own_copy(one).start()

        enter(two, False)

        @pl.when(m == 0)
        def _():
            details(0, one)

    with jax.named_scope("last_details"):
        details(1, two)

        @pl.when(later & (core == 1))
        def _():
            own_copy(one).start()

    with jax.named_scope("pole_sum"):
        mine = pl.ds(pl.multiple_of(me * PART, 8), PART)
        for k in range(2):
            acc = dens[k, mine]
            for step in range(1, 8):
                send_part(k, step).wait_recv()
                acc = acc + parts[k, step - 1]
            total[k, mine] = acc
            for copy in first_totals(k):
                copy.start()
    with jax.named_scope("pole_gather"):
        def pass_on(k, step):
            return send_total(k, lax.rem(me + 8 - step, 8), sibling, step)

        for k in range(2):
            for step in (2, 6, 4):
                send_total(k, lax.rem(me + 8 - step, 8), me, step - 1).wait_recv()
                pass_on(k, step).start()
        for k in range(2):
            send_total(k, sibling, me, 0).wait_recv()
            for step in (2, 6, 4):
                send_total(k, lax.rem(sibling + 8 - step, 8), me, step).wait_recv()
            off_ref[k, :, 0:H] = total[k, 0:W]
            off_ref[k, :, H:W] = total[k, W : 2 * W]
            diag_ref[k] = unpack(total.at[k, pl.ds(2 * W, PACK)])

    def body(p):
        @pl.when(composing & (first_sender(p) | (second(p) & second_sender(p))))
        def _():
            for copy in step_copies(p, 0):
                copy.wait_send()

        @pl.when(lower & head(p))
        def _():
            for copy in step_copies(p, 2):
                copy.wait_send()

        @pl.when((quads & head(p)) | ((m == 0) & (g == 3)))
        def _():
            for when, copy in head_copies(p, head_out):
                pl.when(when)(copy.wait_send)

        for when, copy in relay_copies(p):
            pl.when(when)(copy.wait_send)

        @pl.when(composing & ((plus(p) & (g == 1)) | (~plus(p) & (g == 0))))
        def _():
            pair_copy(p, 1).wait_send()

        @pl.when(passes(p) & ((m > 0) | (g < 3)))
        def _():
            own_copy(p).wait_send()

    both(body)
    for k in range(2):
        for step in range(1, 8):
            send_part(k, step).wait_send()
        for copy in first_totals(k):
            copy.wait_send()
        for step in (2, 6, 4):
            pass_on(k, step).wait_send()


def local(nodes, pivot_inverse, factor_block, live_width_array, pole_weight):
    vmem = pl.BlockSpec(memory_space=pltpu.VMEM)
    hbm = pl.BlockSpec(memory_space=pltpu.HBM)
    dma = pltpu.SemaphoreType.DMA
    packed = pltpu.VMEM((2, 2, PACK, H), F32)
    return pl.pallas_call(
        functools.partial(kernel, nodes),
        out_shape=[jax.ShapeDtypeStruct((2, W, W), F32)] * 2,
        in_specs=[hbm, hbm, hbm, hbm],
        out_specs=[vmem, vmem],
        scratch_shapes=[
            pltpu.VMEM((2, 2, 2, W, W), F32),
            pltpu.VMEM((2, 2, 2, W, W), F32),
            pltpu.SMEM((2,), jnp.int32),
            pltpu.SMEM((2, 2), F32),
            pltpu.VMEM((2, 2, 4, W, W), BF),
            pltpu.VMEM((2, 9, 4, W, W), BF),
            pltpu.VMEM((2, 9, 2, W, W), F32),
            pltpu.VMEM((2, 3, 2, W, W), F32),
            pltpu.VMEM((2, 3, 2, PACK, H), F32),
            pltpu.VMEM((2, 2, 2, W, W), F32),
            pltpu.VMEM((2, 2, 2, PACK, H), F32),
            packed,
            packed,
            packed,
            packed,
            packed,
            pltpu.VMEM((2, 2, W, W), F32),
            pltpu.VMEM((2, ROWS, H), F32),
            pltpu.VMEM((2, 7, PART, H), F32),
            pltpu.VMEM((2, ROWS, H), F32),
            pltpu.VMEM((PACK, H), F32),
            dma((6,)),
            dma((2, 10)),
            dma((2, 8)),
            dma((2, 7)),
            dma((2, 7)),
            dma((2, 7)),
            dma((2, 7)),
        ],
        compiler_params=pltpu.CompilerParams(
            collective_id=0, has_side_effects=True, vmem_limit_bytes=VMEM_MIB << 20
        ),
        name="selected_inversion",
    )(live_width_array, pole_weight, pivot_inverse, factor_block)


def solution(mesh):
    placed = (
        P("pole", "snode", None, None, None),
        P("pole", "snode", None, None, None),
        P("snode"),
        P("pole", None),
    )
    return jax.shard_map(
        functools.partial(local, mesh.shape["snode"]),
        mesh=mesh,
        in_specs=placed,
        out_specs=(P("snode", None, None), P("snode", None, None)),
        check_vma=False,
    )
```
